128 devices in a mesh: gx: 8 (over x, y_lo), gy: 16 (over z, y_hi, core).
Axes of the slice: x: 4, y: 4 (y_hi: 2, y_lo: 2; y = y_hi * 2 + y_lo), z: 4, core: 2. Of those that a mesh axis runs over, the one named last changes fastest.
Arguments:
- activation: bfloat16 [128, 64, 128, 128], P(None, 'gx', 'gy'), may hold values from -6 to 6
- cotangent: bfloat16 [128, 64, 128, 128], P(None, 'gx', 'gy'), may hold values from -6 to 6
- in_factor: bfloat16 [128, 32], replicated, may hold values from -0.5 to 0.5
- core: bfloat16 [3, 3, 3, 32, 32], replicated, may hold values from -0.21875 to 0.21875
- out_factor: bfloat16 [128, 32], replicated, may hold values from -1 to 1
Outputs:
- grad_activation: bfloat16 [128, 64, 128, 128], P(None, 'gx', 'gy')
- grad_in_factor: float32 [128, 32], replicated
- grad_core: float32 [3, 3, 3, 32, 32], replicated
- grad_out_factor: float32 [128, 32], replicated
The draws below stay inside these ranges and needn't reach their ends.
All inputs are finite; a program needn't handle non-finite values.
Results may differ from the reference program's by a relative error of at most 0.0065.
Values may be sent and summed in bfloat16 or wider, within the bound.
A program may use at most 128 MiB of HBM per device.

```python
import jax
import jax.numpy as jnp
from jax import lax

C = 128
R1 = 32
R2 = 32
NZ = 128
NX = 64
NY = 128


def level_of(stream_key, extent, split, least, top_value):
    gain = 1.0
    for position, shards_of in split:
        heights = jax.random.uniform(jax.random.fold_in(jax.random.fold_in(stream_key, 6), position), (shards_of,), jnp.float32, least / len(split), top_value / len(split))
        gain = gain * jnp.repeat(jnp.exp(heights), extent[position] // shards_of).reshape((-1,) + (1,) * (len(extent) - 1 - position))
    return gain


def gaussian(own_key, extent, deviation, limit, pieces=(), kind=jnp.bfloat16):
    gain = level_of(own_key, extent, pieces, -0.22, 0.18) if pieces else 1.0
    result = jax.random.normal(own_key, extent, jnp.float32) * deviation * gain
    return jnp.minimum(jnp.maximum(result, -limit), limit).astype(kind)


def setup_inputs(seed: int = 0) -> dict:
    key_of = jax.random.split(jax.random.key(seed), 6)
    return {
        "activation": gaussian(key_of[0], (C, NX, NY, NZ), 1.0, 6.0, ((1, 8), (2, 16))),
        "cotangent": gaussian(key_of[1], (C, NX, NY, NZ), 1.0, 6.0, ((1, 8), (2, 16))),
        "in_factor": gaussian(key_of[2], (C, R1), C ** -0.5, 0.5),
        "core": gaussian(key_of[3], (3, 3, 3, R2, R1), (27 * R1) ** -0.5, 0.21875),
        "out_factor": gaussian(key_of[4], (C, R2), R2 ** -0.5, 1.0),
    }


def take_z(field, offset):
    size = field.shape[-1]
    if offset == 0:
        return field
    widths = [(0, 0)] * (field.ndim - 1)
    if offset > 0:
        return jnp.pad(field[..., offset:], widths + [(0, offset)])
    return jnp.pad(field[..., :size + offset], widths + [(-offset, 0)])


def shifted(padded, a, b, e, cells_x, cells_y):
    return take_z(padded[:, a:a + cells_x, b:b + cells_y], e - 1)


def reference(activation, cotangent, in_factor, core, out_factor):
    chans, cells_x, cells_y, planes = activation.shape
    rank_in = in_factor.shape[1]
    rank_out = out_factor.shape[1]
    flat_act = activation.reshape(chans, -1)
    flat_cot = cotangent.reshape(chans, -1)
    reduced = jnp.dot(in_factor.T, flat_act, preferred_element_type=jnp.float32).astype(jnp.bfloat16)
    reduced = reduced.reshape(rank_in, cells_x, cells_y, planes)
    padded = jnp.pad(reduced, ((0, 0), (1, 1), (1, 1), (0, 0)))
    total = jnp.zeros((rank_out, cells_x * cells_y * planes), jnp.float32)
    for a in range(3):
        for b in range(3):
            for e in range(3):
                piece = shifted(padded, a, b, e, cells_x, cells_y).reshape(rank_in, -1)
                total = total + jnp.dot(core[a, b, e], piece, preferred_element_type=jnp.float32)
    mixed = total.astype(jnp.bfloat16)
    grad_mixed = jnp.dot(out_factor.T, flat_cot, preferred_element_type=jnp.float32).astype(jnp.bfloat16)
    grad_out_factor = jnp.dot(flat_cot, mixed.T, preferred_element_type=jnp.float32)
    grad_pad = jnp.pad(grad_mixed.reshape(rank_out, cells_x, cells_y, planes), ((0, 0), (1, 1), (1, 1), (0, 0)))
    core_terms = []
    back = jnp.zeros((rank_in, cells_x * cells_y * planes), jnp.float32)
    for a in range(3):
        for b in range(3):
            for e in range(3):
                piece = shifted(padded, a, b, e, cells_x, cells_y).reshape(rank_in, -1)
                core_terms.append(jnp.dot(grad_mixed, piece.T, preferred_element_type=jnp.float32))
                other = shifted(grad_pad, 2 - a, 2 - b, 2 - e, cells_x, cells_y).reshape(rank_out, -1)
                back = back + jnp.dot(core[a, b, e].T, other, preferred_element_type=jnp.float32)
    grad_core = jnp.stack(core_terms).reshape(3, 3, 3, rank_out, rank_in)
    grad_reduced = back.astype(jnp.bfloat16)
    grad_in_factor = jnp.dot(flat_act, grad_reduced.T, preferred_element_type=jnp.float32)
    rows = grad_reduced.reshape(rank_in, cells_x, cells_y * planes).transpose(1, 0, 2)

    def one_row(row):
        return jnp.dot(in_factor, row, preferred_element_type=jnp.float32).astype(jnp.bfloat16)

    grad_rows = lax.map(one_row, rows)
    grad_activation = grad_rows.transpose(1, 0, 2).reshape(chans, cells_x, cells_y, planes)
    return grad_activation, grad_in_factor, grad_core, grad_out_factor
```

```python
import functools

import jax
import jax.numpy as jnp
from jax import lax
from jax.experimental import pallas as pl
from jax.experimental.pallas import tpu as pltpu
from jax.sharding import PartitionSpec as P

MESH = pl.DeviceIdType.MESH
F32 = jnp.float32
BF16 = jnp.bfloat16
WAYS = ((1, 0), (-1, 0), (0, 1), (0, -1), (1, 1), (1, -1), (-1, 1), (-1, -1))
R = 32
ROWS = 11


def mm(a, b):
    return lax.dot_general(a, b, (((1,), (0,)), ((), ())), preferred_element_type=F32)


def mm_nt(a, b):
    return lax.dot_general(a, b, (((1,), (1,)), ((), ())), preferred_element_type=F32)


def iota(shape, dim):
    return lax.broadcasted_iota(jnp.int32, shape, dim)


def z_copies(v):
    lane = iota(v.shape, 1)
    less = jnp.where(lane == 0, 0.0, pltpu.roll(v, 1, 1))
    more = jnp.where(lane == 127, 0.0, pltpu.roll(v, 127, 1))
    return less.astype(BF16), v.astype(BF16), more.astype(BF16)


def spread(factor_t):
    repeat = (iota((8 * R, R), 0) % R == iota((8 * R, R), 1)).astype(BF16)
    rows = mm(repeat, factor_t).astype(BF16)
    widen = (iota((128, 1024), 1) // 8 == iota((128, 1024), 0)).astype(BF16)
    wide = mm(rows, widen)
    keep = iota((8 * R, 1024), 1) % 8 == iota((8 * R, 1024), 0) // R
    return jnp.where(keep, wide, 0.0).astype(BF16)


def spread_t(factor_t):
    lift = (iota((1024, 128), 0) // 8 == iota((1024, 128), 1)).astype(BF16)
    repeat = (iota((8 * R, R), 0) % R == iota((8 * R, R), 1)).astype(BF16)
    rows = mm(repeat, factor_t).astype(BF16)
    tall = mm_nt(lift, rows)
    keep = iota((1024, 8 * R), 0) % 8 == iota((1024, 8 * R), 1) // R
    return jnp.where(keep, tall, 0.0).astype(BF16)


def fold(g):
    keep = iota(g.shape, 0) % 8 == iota(g.shape, 1) // R
    g = jnp.where(keep, g, 0.0)
    g = g[:, :128] + g[:, 128:]
    g = jnp.sum(g.reshape(128, 8, 128), axis=1)
    g = g + pltpu.roll(g, 64, 1)
    g = g + pltpu.roll(g, 32, 1)
    return jnp.transpose(g)[:R]


def kernel(dims, act, cot, inf, core, outf, gact, gcore, gin, gout,
           act_v, cot_v, a2, c2, xs_r, xs_g, red, gmu, hx_r, hx_g, hy_r, hy_g, hxs, hys,
           t_s, w32, w_f, w_b, y32, wk_i, wk_o, wk_t, acc_m, acc_b, part, rs_recv, y_buf, y_recv, fin, gact_v,
           in_sem, out_sem, send_sem, recv_sem, ar_sem):
    n_gx, n_gy = dims
    n_x, n_z = n_gx // 2, n_gy // 4
    group = n_x * n_z * 2
    per = R // group
    gx, gy = lax.axis_index("gx"), lax.axis_index("gy")
    x, y_lo = gx // 2, gx % 2
    z, y_hi, cr = gy // 4, (gy // 2) % 2, gy % 2
    me = (x * n_z + z) * 2 + cr
    my_y = y_hi * 2 + y_lo

    def by_group(j):
        return (j // (2 * n_z)) * 2 + y_lo, ((j // 2) % n_z) * 4 + y_hi * 2 + j % 2

    def by_y(j):
        return x * 2 + j % 2, z * 4 + (j // 2) * 2 + cr

    pairs = ((0, 7), (1, 2), (3, 4), (5, 6))
    loads = []
    for n, (src, dst) in enumerate(((cot, cot_v), (act, act_v))):
        mine = []
        for p in pairs:
            for xx in p:
                c = pltpu.make_async_copy(src.at[:, xx], dst.at[:, xx], in_sem.at[n, xx])
                c.start()
                mine.append(c)
        loads.append(mine)

    for ref in (hx_r, hx_g, hy_r, hy_g):
        ref[...] = jnp.zeros(ref.shape, BF16)
    barrier = pltpu.get_barrier_semaphore()
    for dx, dy in WAYS:
        pl.semaphore_signal(barrier, inc=1, device_id=((gx + dx + n_gx) % n_gx, (gy + dy + n_gy) % n_gy), device_id_type=MESH)

    def greet_group(k, c):
        pl.semaphore_signal(barrier, inc=1, device_id=by_group((me + k) % group), device_id_type=MESH)
        return c

    lax.fori_loop(1, group, greet_group, 0)
    for k in range(1, 4):
        pl.semaphore_signal(barrier, inc=1, device_id=by_y((my_y + k) % 4), device_id_type=MESH)

    wk_o[...] = spread(outf[...])
    wk_i[...] = spread(inf[...])
    for ref in (xs_r, red):
        ref[:, 0:128] = jnp.zeros((ref.shape[0], 128), BF16)
        ref[:, 1152:1280] = jnp.zeros((ref.shape[0], 128), BF16)
    xs_g[:, 0:128] = jnp.zeros((768, 128), BF16)
    xs_g[:, 1152:1280] = jnp.zeros((768, 128), BF16)
    red[0:32, 128:1152] = jnp.zeros((32, 1024), BF16)
    red[288:320, 128:1152] = jnp.zeros((32, 1024), BF16)

    def inside(gxx, gyy):
        return (gxx >= 0) & (gxx < n_gx) & (gyy >= 0) & (gyy < n_gy)

    def send_copy(field, way):
        dx, dy = WAYS[way]
        src, row0, lane0, hx, hy = (gmu, 0, 0, hx_g, hy_g) if field == 0 else (red, 32, 128, hx_r, hy_r)
        edge_x = lane0 + (896 if dx > 0 else 0)
        edge_y = row0 + (224 if dy > 0 else 0)
        if dy == 0:
            s = src.at[pl.ds(row0, 256), pl.ds(edge_x, 128)]
            d = hx.at[0 if dx > 0 else 1, pl.ds(32, 256), :]
        elif dx == 0:
            s = src.at[pl.ds(edge_y, 32), pl.ds(lane0, 1024)]
            d = hy.at[0 if dy > 0 else 1, :, pl.ds(128, 1024)]
        else:
            s = src.at[pl.ds(edge_y, 32), pl.ds(edge_x, 128)]
            d = hy.at[0 if dy > 0 else 1, :, pl.ds(0 if dx > 0 else 1152, 128)]
        return pltpu.make_async_remote_copy(
            src_ref=s, dst_ref=d, send_sem=send_sem.at[field, way], recv_sem=recv_sem.at[field, way],
            device_id=((gx + dx + n_gx) % n_gx, (gy + dy + n_gy) % n_gy), device_id_type=MESH)

    def send(field, way):
        dx, dy = WAYS[way]

        @pl.when(inside(gx + dx, gy + dy))
        def _():
            send_copy(field, way).start()

    def arrive(field, way):
        dx, dy = WAYS[way]

        @pl.when(inside(gx - dx, gy - dy))
        def _():
            send_copy(field, way).wait_recv()

    def sent(field, way):
        dx, dy = WAYS[way]

        @pl.when(inside(gx + dx, gy + dy))
        def _():
            send_copy(field, way).wait_send()

    for field, (raw, flat, wk, xs) in enumerate(((cot_v, c2, wk_o, xs_g), (act_v, a2, wk_i, xs_r))):
        for n, p in enumerate(pairs):
            for side, xx in enumerate(p):
                loads[field][2 * n + side].wait()
                flat[:, xx * 128:xx * 128 + 128] = raw[:, xx].astype(F32).reshape(1024, 128).astype(BF16)
            both = jnp.concatenate([flat[:, xx * 128:xx * 128 + 128] for xx in p], axis=1)
            r = mm(wk[...], both)
            for side, xx in enumerate(p):
                v = r[:, side * 128:side * 128 + 128].astype(BF16).astype(F32)
                copies = z_copies(v)
                if field == 0:
                    gmu[:, xx * 128:xx * 128 + 128] = copies[1]
                else:
                    red[32:288, xx * 128 + 128:xx * 128 + 256] = copies[1]
                for yy in range(8):
                    for e in range(3):
                        xs[yy * 96 + e * 32:yy * 96 + e * 32 + 32, xx * 128 + 128:xx * 128 + 256] = copies[e][yy * 32:yy * 32 + 32]
            if n == 0:
                if field == 0:
                    pl.semaphore_wait(barrier, 8 + group - 1 + 3)
                send(field, 0)
                send(field, 1)
        for way in range(2, 8):
            send(field, way)

    eye = (iota((R, R), 0) == iota((R, R), 1)).astype(BF16)
    for n, w in enumerate((w_f, w_b)):
        w32[...] = jnp.zeros(w32.shape, F32)
        for a in range(3):
            if n == 0:
                for b in range(3):
                    for e in range(3):
                        t_s[:, (b * 3 + e) * 32:(b * 3 + e) * 32 + 32] = core[a, b, e].astype(F32)
            else:
                blocks = [core[2 - a, 2 - b, 2 - e] for b in range(3) for e in range(3)]
                t_s[:, 0:288] = mm_nt(eye, jnp.concatenate(blocks, axis=0))
            for yy in range(8):
                lo = 96 if yy == 0 else 0
                hi = 192 if yy == 7 else 288
                at = a * 768 + 96 * (yy - 1) + lo
                w32[yy * 32:yy * 32 + 32, at:at + hi - lo] = t_s[:, lo:hi]
            y32[n, 0, :, a * 96:a * 96 + 96] = t_s[:, 0:96]
            y32[n, 1, :, a * 96:a * 96 + 96] = t_s[:, 192:288]
        w[...] = w32[...].astype(BF16)
    wk_t[...] = spread_t(inf[...])

    for w, xs, acc in ((w_b, xs_g, acc_b), (w_f, xs_r, acc_m)):
        for t in range(4):
            k = jnp.concatenate([xs[:, (a + 2 * t) * 128:(a + 2 * t) * 128 + 256] for a in range(3)], axis=0)
            acc[:, t * 256:t * 256 + 256] = mm(w[...], k)
    g = jnp.zeros((192, 384), F32)
    for p in range(4):
        k = jnp.concatenate([red[64 * p:64 * p + 128, a * 128:a * 128 + 1024] for a in range(3)], axis=0)
        g = g + mm_nt(xs_g[192 * p:192 * p + 192, 128:1152], k)
    for a in range(3):
        second = pltpu.roll(g[96:192, a * 128:a * 128 + 128], 96, 1)
        total = g[0:96, a * 128:a * 128 + 128] + second
        for e in range(3):
            part[:, a * 3 + 2 - e, :] = total[e * 32:e * 32 + 32]

    def correct(n, field, hx, hy, w, acc):
        for way in range(8):
            arrive(field, way)
        for side in range(2):
            copies = z_copies(hx[side, 32:288, :].astype(F32))
            for yy in range(8):
                for e in range(3):
                    hxs[side, yy * 96 + e * 32:yy * 96 + e * 32 + 32, :] = copies[e][yy * 32:yy * 32 + 32]
            for xp in range(10):
                copies = z_copies(hy[side, :, xp * 128:xp * 128 + 128].astype(F32))
                for e in range(3):
                    hys[side, e * 32:e * 32 + 32, xp * 128:xp * 128 + 128] = copies[e]
        for side in range(2):
            at = 896 * side
            acc[:, at:at + 128] += mm(w[:, 1536 * side:1536 * side + 768], hxs[side])
            k = jnp.concatenate([hys[side, :, a * 128:a * 128 + 1024] for a in range(3)], axis=0)
            acc[224 * side:224 * side + 32, :] += mm(y32[n, side, :, 0:288].astype(BF16), k)
        return acc[...].astype(BF16)

    gr = correct(1, 0, hx_g, hy_g, w_b, acc_b)
    part[:, 10, :] = fold(mm_nt(a2[...], gr))
    mixed = correct(0, 1, hx_r, hy_r, w_f, acc_m)
    part[:, 9, :] = fold(mm_nt(c2[...], mixed))

    gx0 = sum(mm_nt(xs_g[192 * p:192 * p + 192, 128:256], hx_r[0, 64 * p:64 * p + 128, :]) for p in range(4))
    gx2 = sum(mm_nt(xs_g[192 * p:192 * p + 192, 1024:1152], hx_r[1, 64 * p:64 * p + 128, :]) for p in range(4))
    gys = []
    for side in range(2):
        k = jnp.concatenate([hy_r[side, :, a * 128:a * 128 + 1024] for a in (0, 1, 2, 2)], axis=0)
        gys.append(mm_nt(xs_g[672 * side:672 * side + 96, 128:1152], k))
    lane = iota((96, 128), 1)
    for a in range(3):
        total = jnp.where(lane < 32, pltpu.roll(gys[0], (128 - 32 * a) % 128, 1), 0.0)
        total = total + jnp.where((lane >= 64) & (lane < 96), pltpu.roll(gys[1], (192 - 32 * a) % 128, 1), 0.0)
        if a != 1:
            gxx = gx0 if a == 0 else gx2
            total = total + gxx[0:96] + pltpu.roll(gxx[96:192], 96, 1)
        for e in range(3):
            part[:, a * 3 + 2 - e, :] += total[e * 32:e * 32 + 32]

    def rs(k):
        j = (me + k) % group
        return pltpu.make_async_remote_copy(
            src_ref=part.at[pl.ds(j * per, per)], dst_ref=rs_recv.at[k - 1], send_sem=ar_sem.at[0], recv_sem=ar_sem.at[1],
            device_id=by_group(j), device_id_type=MESH)

    def start_rs(k, c):
        rs(k).start()
        return c

    lax.fori_loop(1, group, start_rs, 0)

    outs = []
    for t in range(4):
        r = mm(wk_t[...], gr[:, t * 256:t * 256 + 256])
        for side in range(2):
            xx = 2 * t + side
            gact_v[:, xx] = r[:, side * 128:side * 128 + 128].reshape(128, 8, 128).astype(BF16)
        c = pltpu.make_async_copy(gact_v.at[:, pl.ds(2 * t, 2)], gact.at[:, pl.ds(2 * t, 2)], out_sem.at[t])
        c.start()
        outs.append(c)

    def wait_all(ref, sem):
        pltpu.make_async_copy(ref, ref, sem).wait()

    wait_all(rs_recv, ar_sem.at[1])
    y_buf[...] = part[pl.ds(me * per, per)] + jnp.sum(rs_recv[...], axis=0)
    across = []
    for k in range(1, 4):
        c = pltpu.make_async_remote_copy(
            src_ref=y_buf, dst_ref=y_recv.at[k - 1], send_sem=ar_sem.at[2], recv_sem=ar_sem.at[3],
            device_id=by_y((my_y + k) % 4), device_id_type=MESH)
        c.start()
    wait_all(y_recv, ar_sem.at[3])
    s = jnp.zeros(y_buf.shape, F32)
    for j in range(4):
        slot = (my_y - j + 4) % 4
        other = y_recv[jnp.maximum(slot - 1, 0)]
        s = s + jnp.where(slot == 0, y_buf[...], other)
    fin[pl.ds(me * per, per)] = s

    def ag(k):
        j = (me + k) % group
        return pltpu.make_async_remote_copy(
            src_ref=fin.at[pl.ds(me * per, per)], dst_ref=fin.at[pl.ds(me * per, per)], send_sem=ar_sem.at[4], recv_sem=ar_sem.at[5],
            device_id=by_group(j), device_id_type=MESH)

    def start_ag(k, c):
        ag(k).start()
        return c

    lax.fori_loop(1, group, start_ag, 0)
    wait_all(rs_recv, ar_sem.at[5])
    for a in range(3):
        for e in range(3):
            v = fin[:, a * 3 + e, :]
            for b in range(3):
                gcore[a, b, e] = v[:, b * 32:b * 32 + 32]
    gout[...] = fin[:, 9, :]
    gin[...] = fin[:, 10, :]
    wait_all(rs_recv, ar_sem.at[0])
    wait_all(y_recv, ar_sem.at[2])
    wait_all(rs_recv, ar_sem.at[4])
    for field in range(2):
        for way in range(8):
            sent(field, way)
    for c in outs:
        c.wait()


def shards(dims, activation, cotangent, in_factor, core, out_factor):
    n_gx, n_gy = dims
    group = n_gx * n_gy // 4
    per = R // group
    vm = pl.BlockSpec(memory_space=pltpu.VMEM)
    hbm = pl.BlockSpec(memory_space=pl.ANY)
    gact, gcore, gin, gout = pl.pallas_call(
        functools.partial(kernel, dims),
        out_shape=(
            jax.ShapeDtypeStruct(activation.shape, BF16),
            jax.ShapeDtypeStruct((3, 3, 3, R, R), F32),
            jax.ShapeDtypeStruct((R, 128), F32),
            jax.ShapeDtypeStruct((R, 128), F32),
        ),
        in_specs=[hbm, hbm, vm, vm, vm],
        out_specs=(hbm, vm, vm, vm),
        scratch_shapes=[
            pltpu.VMEM((128, 8, 8, 128), BF16),
            pltpu.VMEM((128, 8, 8, 128), BF16),
            pltpu.VMEM((1024, 1024), BF16),
            pltpu.VMEM((1024, 1024), BF16),
            pltpu.VMEM((768, 1280), BF16),
            pltpu.VMEM((768, 1280), BF16),
            pltpu.VMEM((320, 1280), BF16),
            pltpu.VMEM((256, 1024), BF16),
            pltpu.VMEM((2, 320, 128), BF16),
            pltpu.VMEM((2, 320, 128), BF16),
            pltpu.VMEM((2, 32, 1280), BF16),
            pltpu.VMEM((2, 32, 1280), BF16),
            pltpu.VMEM((2, 768, 128), BF16),
            pltpu.VMEM((2, 96, 1280), BF16),
            pltpu.VMEM((32, 384), F32),
            pltpu.VMEM((256, 2304), F32),
            pltpu.VMEM((256, 2304), BF16),
            pltpu.VMEM((256, 2304), BF16),
            pltpu.VMEM((2, 2, 32, 384), F32),
            pltpu.VMEM((256, 1024), BF16),
            pltpu.VMEM((256, 1024), BF16),
            pltpu.VMEM((1024, 256), BF16),
            pltpu.VMEM((256, 1024), F32),
            pltpu.VMEM((256, 1024), F32),
            pltpu.VMEM((R, ROWS, 128), F32),
            pltpu.VMEM((group - 1, per, ROWS, 128), F32),
            pltpu.VMEM((per, ROWS, 128), F32),
            pltpu.VMEM((3, per, ROWS, 128), F32),
            pltpu.VMEM((R, ROWS, 128), F32),
            pltpu.VMEM((128, 8, 8, 128), BF16),
            pltpu.SemaphoreType.DMA((2, 8)),
            pltpu.SemaphoreType.DMA((4,)),
            pltpu.SemaphoreType.DMA((2, 8)),
            pltpu.SemaphoreType.DMA((2, 8)),
            pltpu.SemaphoreType.DMA((6,)),
        ],
        compiler_params=pltpu.CompilerParams(collective_id=0, has_side_effects=True, vmem_limit_bytes=56 * 1024 * 1024),
    )(activation, cotangent, in_factor.T, core, out_factor.T)
    return gact, gin.T, gcore, gout.T


def solution(mesh):
    dims = (mesh.shape["gx"], mesh.shape["gy"])
    placed = (P(None, "gx", "gy", None), P(None, "gx", "gy", None), P(), P(), P())
    return jax.shard_map(
        functools.partial(shards, dims),
        mesh=mesh,
        in_specs=placed,
        out_specs=(P(None, "gx", "gy", None), P(), P(), P()),
        check_vma=False,
    )
```

```python
import functools

import jax
import jax.numpy as jnp
from jax import lax
from jax.experimental import pallas as pl
from jax.experimental.pallas import tpu as pltpu
from jax.sharding import PartitionSpec as P

MESH = pl.DeviceIdType.MESH
F32 = jnp.float32
BF16 = jnp.bfloat16
WAYS = ((1, 0), (-1, 0), (0, 1), (0, -1), (1, 1), (1, -1), (-1, 1), (-1, -1))
R = 32
ROWS = 9
HALF = R // 2


def mm(a, b):
    return lax.dot_general(a, b, (((1,), (0,)), ((), ())), preferred_element_type=F32)


def mm_nt(a, b):
    return lax.dot_general(a, b, (((1,), (1,)), ((), ())), preferred_element_type=F32)


def iota(shape, dim):
    return lax.broadcasted_iota(jnp.int32, shape, dim)


def z_copies(v):
    lane = iota(v.shape, 1)
    less = jnp.where(lane == 0, 0.0, pltpu.roll(v, 1, 1))
    more = jnp.where(lane == 127, 0.0, pltpu.roll(v, 127, 1))
    return less.astype(BF16), v.astype(BF16), more.astype(BF16)


def spread(factor_t):
    repeat = (iota((8 * R, R), 0) % R == iota((8 * R, R), 1)).astype(BF16)
    rows = mm(repeat, factor_t).astype(BF16)
    widen = (iota((128, 1024), 1) // 8 == iota((128, 1024), 0)).astype(BF16)
    wide = mm(rows, widen)
    keep = iota((8 * R, 1024), 1) % 8 == iota((8 * R, 1024), 0) // R
    return jnp.where(keep, wide, 0.0).astype(BF16)


def spread_t(factor_t):
    lift = (iota((1024, 128), 0) // 8 == iota((1024, 128), 1)).astype(BF16)
    repeat = (iota((8 * R, R), 0) % R == iota((8 * R, R), 1)).astype(BF16)
    rows = mm(repeat, factor_t).astype(BF16)
    tall = mm_nt(lift, rows)
    keep = iota((1024, 8 * R), 0) % 8 == iota((1024, 8 * R), 1) // R
    return jnp.where(keep, tall, 0.0).astype(BF16)


def fold(g):
    keep = iota(g.shape, 0) % 8 == iota(g.shape, 1) // R
    g = jnp.where(keep, g, 0.0)
    g = g[:, :128] + g[:, 128:]
    g = jnp.sum(g.reshape(128, 8, 128), axis=1)
    g = g + pltpu.roll(g, 64, 1)
    g = g + pltpu.roll(g, 32, 1)
    return jnp.transpose(g)[:R]


def kernel(dims, act, cot, inf, core, outf, gact_v, gcore, gin, gout,
           act_v, cot_v, a2, c2, xs_r, xs_g, red, gmu, hx_r, hx_g, hy_r, hy_g, hxs, hys,
           t_s, w32, w_f, w_b, y32, wk_i, wk_o, wk_t, acc_m, acc_b, own, part, rs_recv, y_recv, fin, part2, c_recv, xz_recv, y2_recv,
           in_sem, send_sem, recv_sem, ar_sem, f_sem):
    n_gx, n_gy = dims
    n_x, n_z = n_gx // 2, n_gy // 4
    group = n_x * n_z * 2
    per = R // group
    gx, gy = lax.axis_index("gx"), lax.axis_index("gy")
    x, y_lo = gx // 2, gx % 2
    z, y_hi, cr = gy // 4, (gy // 2) % 2, gy % 2
    me = (x * n_z + z) * 2 + cr
    my_y = y_hi * 2 + y_lo

    def by_group(j):
        return (j // (2 * n_z)) * 2 + y_lo, ((j // 2) % n_z) * 4 + y_hi * 2 + j % 2

    def by_y(j):
        return x * 2 + j % 2, z * 4 + (j // 2) * 2 + cr

    pairs = ((0, 7), (1, 2), (3, 4), (5, 6))
    loads = []
    for n, (src, dst) in enumerate(((cot, cot_v), (act, act_v))):
        mine = []
        for k, xx in enumerate((pl.ds(0, 1), pl.ds(7, 1), pl.ds(1, 6))):
            c = pltpu.make_async_copy(src.at[:, xx], dst.at[:, xx], in_sem.at[n, k])
            c.start()
            mine.append(c)
        loads.append(mine)

    for ref in (hx_r, hx_g, hy_r, hy_g):
        ref[...] = jnp.zeros(ref.shape, BF16)
    barrier = pltpu.get_barrier_semaphore()
    for dx, dy in WAYS:
        pl.semaphore_signal(barrier, inc=1, device_id=((gx + dx + n_gx) % n_gx, (gy + dy + n_gy) % n_gy), device_id_type=MESH)

    def greet_group(k, c):
        pl.semaphore_signal(barrier, inc=1, device_id=by_group((me + k) % group), device_id_type=MESH)
        return c

    lax.fori_loop(1, group, greet_group, 0)
    for k in range(1, 4):
        pl.semaphore_signal(barrier, inc=1, device_id=by_y((my_y + k) % 4), device_id_type=MESH)

    wk_o[...] = spread(outf[...])
    wk_i[...] = spread(inf[...])
    for ref in (xs_r, red):
        ref[:, 0:128] = jnp.zeros((ref.shape[0], 128), BF16)
        ref[:, 1152:1280] = jnp.zeros((ref.shape[0], 128), BF16)
    xs_g[:, 0:128] = jnp.zeros((768, 128), BF16)
    xs_g[:, 1152:1280] = jnp.zeros((768, 128), BF16)
    red[0:32, 128:1152] = jnp.zeros((32, 1024), BF16)
    red[288:320, 128:1152] = jnp.zeros((32, 1024), BF16)

    def inside(gxx, gyy):
        return (gxx >= 0) & (gxx < n_gx) & (gyy >= 0) & (gyy < n_gy)

    def send_copy(field, way):
        dx, dy = WAYS[way]
        src, row0, lane0, hx, hy = (gmu, 0, 0, hx_g, hy_g) if field == 0 else (red, 32, 128, hx_r, hy_r)
        edge_x = lane0 + (896 if dx > 0 else 0)
        edge_y = row0 + (224 if dy > 0 else 0)
        if dy == 0:
            s = src.at[pl.ds(row0, 256), pl.ds(edge_x, 128)]
            d = hx.at[0 if dx > 0 else 1]
        elif dx == 0:
            s = src.at[pl.ds(edge_y, 32), pl.ds(lane0, 1024)]
            d = hy.at[0 if dy > 0 else 1, :, pl.ds(128, 1024)]
        else:
            s = src.at[pl.ds(edge_y, 32), pl.ds(edge_x, 128)]
            d = hy.at[0 if dy > 0 else 1, :, pl.ds(0 if dx > 0 else 1152, 128)]
        return pltpu.make_async_remote_copy(
            src_ref=s, dst_ref=d, send_sem=send_sem.at[field, way], recv_sem=recv_sem.at[field, way],
            device_id=((gx + dx + n_gx) % n_gx, (gy + dy + n_gy) % n_gy), device_id_type=MESH)

    def send(field, way):
        dx, dy = WAYS[way]

        @pl.when(inside(gx + dx, gy + dy))
        def _():
            send_copy(field, way).start()

    def arrive(field, way):
        dx, dy = WAYS[way]

        @pl.when(inside(gx - dx, gy - dy))
        def _():
            send_copy(field, way).wait_recv()

    def sent(field, way):
        dx, dy = WAYS[way]

        @pl.when(inside(gx + dx, gy + dy))
        def _():
            send_copy(field, way).wait_send()

    for field, (raw, flat, wk, xs) in enumerate(((cot_v, c2, wk_o, xs_g), (act_v, a2, wk_i, xs_r))):
        for n, p in enumerate(pairs):
            for c in loads[field][0:2] if n == 0 else loads[field][2:3] if n == 1 else ():
                c.wait()
            for xx in p:
                flat[:, xx * 128:xx * 128 + 128] = raw[:, xx].astype(F32).reshape(1024, 128).astype(BF16)
            both = jnp.concatenate([flat[:, xx * 128:xx * 128 + 128] for xx in p], axis=1)
            r = mm(wk[...], both)
            for side, xx in enumerate(p):
                v = r[:, side * 128:side * 128 + 128].astype(BF16).astype(F32)
                copies = z_copies(v)
                if field == 0:
                    gmu[:, xx * 128:xx * 128 + 128] = copies[1]
                else:
                    red[32:288, xx * 128 + 128:xx * 128 + 256] = copies[1]
                for yy in range(8):
                    for e in range(3):
                        xs[yy * 96 + e * 32:yy * 96 + e * 32 + 32, xx * 128 + 128:xx * 128 + 256] = copies[e][yy * 32:yy * 32 + 32]
            if n == 0:
                if field == 0:
                    pl.semaphore_wait(barrier, 8 + group - 1 + 3)
                send(field, 0)
                send(field, 1)
        for way in range(2, 8):
            send(field, way)

    eye = (iota((R, R), 0) == iota((R, R), 1)).astype(BF16)
    for n, w in enumerate((w_f, w_b)):
        w32[...] = jnp.zeros(w32.shape, F32)
        for a in range(3):
            if n == 0:
                for b in range(3):
                    for e in range(3):
                        t_s[:, (b * 3 + e) * 32:(b * 3 + e) * 32 + 32] = core[a, b, e].astype(F32)
            else:
                blocks = [core[2 - a, 2 - b, 2 - e] for b in range(3) for e in range(3)]
                t_s[:, 0:288] = mm_nt(eye, jnp.concatenate(blocks, axis=0))
            for yy in range(8):
                lo = 96 if yy == 0 else 0
                hi = 192 if yy == 7 else 288
                at = a * 768 + 96 * (yy - 1) + lo
                w32[yy * 32:yy * 32 + 32, at:at + hi - lo] = t_s[:, lo:hi]
            y32[n, 0, :, a * 96:a * 96 + 96] = t_s[:, 0:96]
            y32[n, 1, :, a * 96:a * 96 + 96] = t_s[:, 192:288]
        w[...] = w32[...].astype(BF16)
    wk_t[...] = spread_t(inf[...])

    for w, xs, acc in ((w_b, xs_g, acc_b), (w_f, xs_r, acc_m)):
        for t in range(4):
            k = jnp.concatenate([xs[:, (a + 2 * t) * 128:(a + 2 * t) * 128 + 256] for a in range(3)], axis=0)
            acc[:, t * 256:t * 256 + 256] = mm(w[...], k)
    g = jnp.zeros((192, 384), F32)
    for p in range(4):
        k = jnp.concatenate([red[64 * p:64 * p + 128, a * 128:a * 128 + 1024] for a in range(3)], axis=0)
        g = g + mm_nt(xs_g[192 * p:192 * p + 192, 128:1152], k)
    for a in range(3):
        second = pltpu.roll(g[96:192, a * 128:a * 128 + 128], 96, 1)
        own[a] = g[0:96, a * 128:a * 128 + 128] + second

    def halo_copies(field, hx, hy):
        for way in range(8):
            arrive(field, way)
        for side in range(2):
            copies = z_copies(hx[side].astype(F32))
            for yy in range(8):
                for e in range(3):
                    hxs[side, yy * 96 + e * 32:yy * 96 + e * 32 + 32, :] = copies[e][yy * 32:yy * 32 + 32]
            for xp in range(10):
                copies = z_copies(hy[side, :, xp * 128:xp * 128 + 128].astype(F32))
                for e in range(3):
                    hys[side, e * 32:e * 32 + 32, xp * 128:xp * 128 + 128] = copies[e]

    def correct(n, w, acc):
        for side in range(2):
            at = 896 * side
            acc[:, at:at + 128] += mm(w[:, 1536 * side:1536 * side + 768], hxs[side])
            k = jnp.concatenate([hys[side, :, a * 128:a * 128 + 1024] for a in range(3)], axis=0)
            acc[224 * side:224 * side + 32, :] += mm(y32[n, side, :, 0:288].astype(BF16), k)
        return acc[...].astype(BF16)

    halo_copies(0, hx_g, hy_g)
    g_x = []
    for side in range(2):
        lanes = pl.ds(128 + 896 * side, 128)
        g_x.append(sum(mm_nt(hxs[side, 192 * p:192 * p + 192, :], red[64 * p:64 * p + 128, lanes]) for p in range(4)))
    g_y = jnp.zeros((288, 128), F32)
    for side in range(2):
        k = jnp.concatenate([hys[side, :, (2 - a) * 128:(2 - a) * 128 + 1024] for a in range(3)], axis=0)
        row = red[32 + 224 * side:64 + 224 * side, 128:1152]
        none = jnp.zeros_like(row)
        row = jnp.concatenate([none, none, row, none] if side == 0 else [row, none, none, none], axis=0)
        g_y = g_y + mm_nt(k, row)
    for a in range(3):
        total = own[a] + g_y[a * 96:a * 96 + 96]
        if a != 1:
            gxx = g_x[0] if a == 2 else g_x[1]
            total = total + gxx[0:96] + pltpu.roll(gxx[96:192], 96, 1)
        for e in range(3):
            part[:, a * 3 + 2 - e, :] = total[e * 32:e * 32 + 32]

    def wait_all(ref, sem):
        pltpu.make_async_copy(ref, ref, sem).wait()

    def start_y(buf, n):
        for k in range(1, 4):
            pltpu.make_async_remote_copy(
                src_ref=buf.at[my_y], dst_ref=buf.at[my_y], send_sem=ar_sem.at[n], recv_sem=ar_sem.at[n + 1],
                device_id=by_y((my_y + k) % 4), device_id_type=MESH).start()

    def start_rs(k, c):
        j = (me + k) % group
        pltpu.make_async_remote_copy(
            src_ref=part.at[pl.ds(j * per, per)], dst_ref=rs_recv.at[k - 1], send_sem=ar_sem.at[0], recv_sem=ar_sem.at[1],
            device_id=by_group(j), device_id_type=MESH).start()
        return c

    def start_ag(k, c):
        pltpu.make_async_remote_copy(
            src_ref=fin.at[pl.ds(me * per, per)], dst_ref=fin.at[pl.ds(me * per, per)], send_sem=ar_sem.at[4], recv_sem=ar_sem.at[5],
            device_id=by_group((me + k) % group), device_id_type=MESH).start()
        return c

    other = (gx, gy + 1 - 2 * cr)
    mine, theirs = pl.ds(pl.multiple_of(cr * HALF, HALF), HALF), pl.ds(pl.multiple_of((1 - cr) * HALF, HALF), HALF)
    plane = n_x * n_z
    at = x * n_z + z
    results = (gin, gout)

    def to_core(n):
        return pltpu.make_async_remote_copy(
            src_ref=part2.at[n, theirs], dst_ref=c_recv.at[n], send_sem=f_sem.at[n, 0], recv_sem=f_sem.at[n, 1],
            device_id=other, device_id_type=MESH)

    def over_xz(n):
        to_core(n).wait_recv()
        xz_recv[n, at] = part2[n, mine] + c_recv[n]

        def start_xz(k, c):
            j = (at + k) % plane
            pltpu.make_async_remote_copy(
                src_ref=xz_recv.at[n, at], dst_ref=xz_recv.at[n, at], send_sem=f_sem.at[n, 2], recv_sem=f_sem.at[n, 3],
                device_id=((j // n_z) * 2 + y_lo, (j % n_z) * 4 + y_hi * 2 + cr), device_id_type=MESH).start()
            return c

        lax.fori_loop(1, plane, start_xz, 0)

    def over_y(n):
        wait_all(xz_recv.at[n, pl.ds(0, plane - 1)], f_sem.at[n, 3])
        y2_recv[n, my_y] = jnp.sum(xz_recv[n], axis=0)
        start_y(y2_recv.at[n], 6 + 2 * n)

    def swap(n):
        return pltpu.make_async_remote_copy(
            src_ref=results[n].at[mine], dst_ref=results[n].at[mine], send_sem=f_sem.at[n, 4], recv_sem=f_sem.at[n, 5],
            device_id=other, device_id_type=MESH)

    def back(n):
        wait_all(y2_recv.at[n, pl.ds(0, 3)], ar_sem.at[7 + 2 * n])
        results[n][mine] = jnp.sum(y2_recv[n], axis=0)
        swap(n).start()

    lax.fori_loop(1, group, start_rs, 0)
    gr = correct(1, w_b, acc_b)
    part2[0] = fold(mm_nt(a2[...], gr))
    to_core(0).start()
    for t in range(4):
        r = mm(wk_t[...], gr[:, t * 256:t * 256 + 256])
        for side in range(2):
            gact_v[:, 2 * t + side] = r[:, side * 128:side * 128 + 128].reshape(128, 8, 128).astype(BF16)
    over_xz(0)

    halo_copies(1, hx_r, hy_r)
    mixed = correct(0, w_f, acc_m)
    part2[1] = fold(mm_nt(c2[...], mixed))
    to_core(1).start()

    wait_all(rs_recv, ar_sem.at[1])
    y_recv[my_y] = part[pl.ds(me * per, per)] + jnp.sum(rs_recv[...], axis=0)
    start_y(y_recv, 2)
    over_xz(1)
    over_y(0)
    wait_all(y_recv.at[pl.ds(0, 3)], ar_sem.at[3])
    fin[pl.ds(me * per, per)] = jnp.sum(y_recv[...], axis=0)
    lax.fori_loop(1, group, start_ag, 0)
    over_y(1)
    back(0)
    back(1)
    wait_all(rs_recv, ar_sem.at[5])
    for a in range(3):
        for e in range(3):
            v = fin[:, a * 3 + e, :]
            for b in range(3):
                gcore[a, b, e] = v[:, b * 32:b * 32 + 32]
    wait_all(rs_recv, ar_sem.at[0])
    wait_all(y_recv.at[pl.ds(0, 3)], ar_sem.at[2])
    wait_all(rs_recv, ar_sem.at[4])
    for n in range(2):
        swap(n).wait_recv()
        to_core(n).wait_send()
        wait_all(xz_recv.at[n, pl.ds(0, plane - 1)], f_sem.at[n, 2])
        wait_all(y2_recv.at[n, pl.ds(0, 3)], ar_sem.at[6 + 2 * n])
        swap(n).wait_send()
    for field in range(2):
        for way in range(8):
            sent(field, way)


def finish(*refs):
    copies = [pltpu.make_async_copy(refs[n], refs[n + 4], refs[8].at[n]) for n in range(4)]
    for c in copies:
        c.start()
    for c in copies:
        c.wait()


def shards(dims, activation, cotangent, in_factor, core, out_factor):
    n_gx, n_gy = dims
    group = n_gx * n_gy // 4
    per = R // group
    vm = pl.BlockSpec(memory_space=pltpu.VMEM)
    hbm = pl.BlockSpec(memory_space=pl.ANY)
    held = pl.pallas_call(
        functools.partial(kernel, dims),
        out_shape=(
            pltpu.VMEM(activation.shape, BF16),
            pltpu.VMEM((3, 3, 3, R, R), F32),
            pltpu.VMEM((R, 128), F32),
            pltpu.VMEM((R, 128), F32),
        ),
        in_specs=[hbm, hbm, vm, vm, vm],
        out_specs=(vm, vm, vm, vm),
        scratch_shapes=[
            pltpu.VMEM((128, 8, 8, 128), BF16),
            pltpu.VMEM((128, 8, 8, 128), BF16),
            pltpu.VMEM((1024, 1024), BF16),
            pltpu.VMEM((1024, 1024), BF16),
            pltpu.VMEM((768, 1280), BF16),
            pltpu.VMEM((768, 1280), BF16),
            pltpu.VMEM((320, 1280), BF16),
            pltpu.VMEM((256, 1024), BF16),
            pltpu.VMEM((2, 256, 128), BF16),
            pltpu.VMEM((2, 256, 128), BF16),
            pltpu.VMEM((2, 32, 1280), BF16),
            pltpu.VMEM((2, 32, 1280), BF16),
            pltpu.VMEM((2, 768, 128), BF16),
            pltpu.VMEM((2, 96, 1280), BF16),
            pltpu.VMEM((32, 384), F32),
            pltpu.VMEM((256, 2304), F32),
            pltpu.VMEM((256, 2304), BF16),
            pltpu.VMEM((256, 2304), BF16),
            pltpu.VMEM((2, 2, 32, 384), F32),
            pltpu.VMEM((256, 1024), BF16),
            pltpu.VMEM((256, 1024), BF16),
            pltpu.VMEM((1024, 256), BF16),
            pltpu.VMEM((256, 1024), F32),
            pltpu.VMEM((256, 1024), F32),
            pltpu.VMEM((3, 96, 128), F32),
            pltpu.VMEM((R, ROWS, 128), F32),
            pltpu.VMEM((group - 1, per, ROWS, 128), F32),
            pltpu.VMEM((4, per, ROWS, 128), F32),
            pltpu.VMEM((R, ROWS, 128), F32),
            pltpu.VMEM((2, R, 128), F32),
            pltpu.VMEM((2, HALF, 128), F32),
            pltpu.VMEM((2, group // 2, HALF, 128), F32),
            pltpu.VMEM((2, 4, HALF, 128), F32),
            pltpu.SemaphoreType.DMA((2, 3)),
            pltpu.SemaphoreType.DMA((2, 8)),
            pltpu.SemaphoreType.DMA((2, 8)),
            pltpu.SemaphoreType.DMA((10,)),
            pltpu.SemaphoreType.DMA((2, 6)),
        ],
        compiler_params=pltpu.CompilerParams(collective_id=0, has_side_effects=True, vmem_limit_bytes=60 * 1024 * 1024),
    )(activation, cotangent, in_factor.T, core, out_factor.T)
    gact, gcore, gin, gout = pl.pallas_call(
        finish,
        out_shape=(
            jax.ShapeDtypeStruct(activation.shape, BF16),
            jax.ShapeDtypeStruct((3, 3, 3, R, R), F32),
            jax.ShapeDtypeStruct((R, 128), F32),
            jax.ShapeDtypeStruct((R, 128), F32),
        ),
        in_specs=[vm] * 4,
        out_specs=(hbm,) * 4,
        scratch_shapes=[pltpu.SemaphoreType.DMA((4,))],
        compiler_params=pltpu.CompilerParams(vmem_limit_bytes=24 * 1024 * 1024),
    )(*held)
    return gact, gin.T, gcore, gout.T


def solution(mesh):
    dims = (mesh.shape["gx"], mesh.shape["gy"])
    placed = (P(None, "gx", "gy", None), P(None, "gx", "gy", None), P(), P(), P())
    return jax.shard_map(
        functools.partial(shards, dims),
        mesh=mesh,
        in_specs=placed,
        out_specs=(P(None, "gx", "gy", None), P(), P(), P()),
        check_vma=False,
    )
```

```python
import functools

import jax
import jax.numpy as jnp
from jax import lax
from jax.experimental import pallas as pl
from jax.experimental.pallas import tpu as pltpu
from jax.sharding import PartitionSpec as P

MESH = pl.DeviceIdType.MESH
F32 = jnp.float32
BF16 = jnp.bfloat16
WAYS = ((1, 0), (-1, 0), (0, 1), (0, -1), (1, 1), (1, -1), (-1, 1), (-1, -1))
R = 32
ROWS = 10
HALF = R // 2


def mm(a, b):
    return lax.dot_general(a, b, (((1,), (0,)), ((), ())), preferred_element_type=F32)


def mm_nt(a, b):
    return lax.dot_general(a, b, (((1,), (1,)), ((), ())), preferred_element_type=F32)


def iota(shape, dim):
    return lax.broadcasted_iota(jnp.int32, shape, dim)


def z_copies(v):
    lane = iota(v.shape, 1)
    less = jnp.where(lane == 0, 0.0, pltpu.roll(v, 1, 1))
    more = jnp.where(lane == 127, 0.0, pltpu.roll(v, 127, 1))
    return less.astype(BF16), v.astype(BF16), more.astype(BF16)


def spread(factor_t):
    repeat = (iota((8 * R, R), 0) % R == iota((8 * R, R), 1)).astype(BF16)
    rows = mm(repeat, factor_t).astype(BF16)
    widen = (iota((128, 1024), 1) // 8 == iota((128, 1024), 0)).astype(BF16)
    wide = mm(rows, widen)
    keep = iota((8 * R, 1024), 1) % 8 == iota((8 * R, 1024), 0) // R
    return jnp.where(keep, wide, 0.0).astype(BF16)


def spread_t(factor_t):
    lift = (iota((1024, 128), 0) // 8 == iota((1024, 128), 1)).astype(BF16)
    repeat = (iota((8 * R, R), 0) % R == iota((8 * R, R), 1)).astype(BF16)
    rows = mm(repeat, factor_t).astype(BF16)
    tall = mm_nt(lift, rows)
    keep = iota((1024, 8 * R), 0) % 8 == iota((1024, 8 * R), 1) // R
    return jnp.where(keep, tall, 0.0).astype(BF16)


def fold(g):
    keep = iota(g.shape, 0) % 8 == iota(g.shape, 1) // R
    g = jnp.where(keep, g, 0.0)
    g = g[:, :128] + g[:, 128:]
    g = jnp.sum(g.reshape(128, 8, 128), axis=1)
    g = g + pltpu.roll(g, 64, 1)
    g = g + pltpu.roll(g, 32, 1)
    return jnp.transpose(g)[:R]


def kernel(dims, act, cot, inf, core, outf, gact_v, gcore, gin, gout,
           act_v, cot_v, a2, c2, xs_r, xs_g, red, gmu, hx_r, hx_g, hy_r, hy_g, hxs, hys,
           t_s, w32, w_f, w_b, y32, wk_i, wk_o, wk_t, acc_m, acc_b, own, part, rs_recv, y_recv, fin, part2, c_recv, xz_recv, y2_recv,
           in_sem, send_sem, recv_sem, ar_sem, f_sem, known):
    n_gx, n_gy = dims
    n_x, n_z = n_gx // 2, n_gy // 4
    group = n_x * n_z * 2
    per = R // group
    gx, gy = lax.axis_index("gx"), lax.axis_index("gy")
    x, y_lo = gx // 2, gx % 2
    z, y_hi, cr = gy // 4, (gy // 2) % 2, gy % 2
    me = (x * n_z + z) * 2 + cr
    my_y = y_hi * 2 + y_lo

    def by_y(j):
        return x * 2 + j % 2, z * 4 + (j // 2) * 2 + cr

    pairs = ((0, 7), (1, 2), (3, 4), (5, 6))
    loads = []
    for n, (src, dst) in enumerate(((cot, cot_v), (act, act_v))):
        mine = []
        for k, xx in enumerate((pl.ds(0, 1), pl.ds(7, 1), pl.ds(1, 6))):
            c = pltpu.make_async_copy(src.at[:, xx], dst.at[:, xx], in_sem.at[n, k])
            c.start()
            mine.append(c)
        loads.append(mine)

    for ref in (hx_r, hx_g, hy_r, hy_g):
        ref[...] = jnp.zeros(ref.shape, BF16)
    barrier = pltpu.get_barrier_semaphore()
    flip = 1 - 2 * cr
    has_up, has_down = z < n_z - 1, z > 0
    first, last = gy == 0, gy == n_gy - 1

    def greet(sem, partners):
        due = 0
        for there, dx, dy in partners:
            who = ((gx + dx + n_gx) % n_gx, gy + dy)
            if there is True:
                pl.semaphore_signal(sem, inc=1, device_id=who, device_id_type=MESH)
                due = due + 1
            else:

                @pl.when(there)
                def _():
                    pl.semaphore_signal(sem, inc=1, device_id=who, device_id_type=MESH)

                due = due + there.astype(jnp.int32)
        return due

    side_l, side_h = 1 - 2 * y_lo, 2 - 4 * y_hi
    up, down = jnp.logical_not(last), jnp.logical_not(first)
    near = [(True if dy == 0 else up if dy > 0 else down, dx, dy) for dx, dy in WAYS]
    near += [(True, dx, dy) for dx in (2, -2) for dy in (0, flip)]
    near += [(has_up, 0, 4), (has_up, 0, 4 + flip), (has_down, 0, -4), (has_down, 0, -4 + flip)]
    near += [(True, side_l, 0), (True, 0, side_h), (True, side_l, side_h)]
    near_due = greet(barrier, near)

    wk_o[...] = spread(outf[...])
    wk_i[...] = spread(inf[...])
    for ref in (xs_r, red):
        ref[:, 0:128] = jnp.zeros((ref.shape[0], 128), BF16)
        ref[:, 1152:1280] = jnp.zeros((ref.shape[0], 128), BF16)
    xs_g[:, 0:128] = jnp.zeros((768, 128), BF16)
    xs_g[:, 1152:1280] = jnp.zeros((768, 128), BF16)
    red[0:32, 128:1152] = jnp.zeros((32, 1024), BF16)
    red[288:320, 128:1152] = jnp.zeros((32, 1024), BF16)

    def inside(gxx, gyy):
        return (gxx >= 0) & (gxx < n_gx) & (gyy >= 0) & (gyy < n_gy)

    def send_copy(field, way):
        dx, dy = WAYS[way]
        src, row0, lane0, hx, hy = (gmu, 0, 0, hx_g, hy_g) if field == 0 else (red, 32, 128, hx_r, hy_r)
        edge_x = lane0 + (896 if dx > 0 else 0)
        edge_y = row0 + (224 if dy > 0 else 0)
        if dy == 0:
            s = src.at[pl.ds(row0, 256), pl.ds(edge_x, 128)]
            d = hx.at[0 if dx > 0 else 1]
        elif dx == 0:
            s = src.at[pl.ds(edge_y, 32), pl.ds(lane0, 1024)]
            d = hy.at[0 if dy > 0 else 1, :, pl.ds(128, 1024)]
        else:
            s = src.at[pl.ds(edge_y, 32), pl.ds(edge_x, 128)]
            d = hy.at[0 if dy > 0 else 1, :, pl.ds(0 if dx > 0 else 1152, 128)]
        return pltpu.make_async_remote_copy(
            src_ref=s, dst_ref=d, send_sem=send_sem.at[field, way], recv_sem=recv_sem.at[field, way],
            device_id=((gx + dx + n_gx) % n_gx, (gy + dy + n_gy) % n_gy), device_id_type=MESH)

    def send(field, way):
        dx, dy = WAYS[way]

        @pl.when(inside(gx + dx, gy + dy))
        def _():
            send_copy(field, way).start()

    def arrive(field, way):
        dx, dy = WAYS[way]

        @pl.when(inside(gx - dx, gy - dy))
        def _():
            send_copy(field, way).wait_recv()

    def sent(field, way):
        dx, dy = WAYS[way]

        @pl.when(inside(gx + dx, gy + dy))
        def _():
            send_copy(field, way).wait_send()

    for field, (raw, flat, wk, xs) in enumerate(((cot_v, c2, wk_o, xs_g), (act_v, a2, wk_i, xs_r))):
        for n, p in enumerate(pairs):
            for c in loads[field][0:2] if n == 0 else loads[field][2:3] if n == 1 else ():
                c.wait()
            for xx in p:
                flat[:, xx * 128:xx * 128 + 128] = raw[:, xx].astype(F32).reshape(1024, 128).astype(BF16)
            both = jnp.concatenate([flat[:, xx * 128:xx * 128 + 128] for xx in p], axis=1)
            r = mm(wk[...], both)
            for side, xx in enumerate(p):
                v = r[:, side * 128:side * 128 + 128].astype(BF16).astype(F32)
                copies = z_copies(v)
                if field == 0:
                    gmu[:, xx * 128:xx * 128 + 128] = copies[1]
                else:
                    red[32:288, xx * 128 + 128:xx * 128 + 256] = copies[1]
                for yy in range(8):
                    for e in range(3):
                        xs[yy * 96 + e * 32:yy * 96 + e * 32 + 32, xx * 128 + 128:xx * 128 + 256] = copies[e][yy * 32:yy * 32 + 32]
            if n == 0:
                if field == 0:
                    pl.semaphore_wait(barrier, near_due)
                    known_due = greet(known.at[0], [(True, 2, 0), (True, -2, 0), (has_up, 0, 4), (has_down, 0, -4)])
                send(field, 0)
                send(field, 1)
        for way in range(2, 8):
            send(field, way)

    pl.semaphore_wait(known.at[0], known_due)
    known_due = greet(known.at[1], [(z < n_z - 2, 0, 8), (z > 1, 0, -8)])

    eye = (iota((R, R), 0) == iota((R, R), 1)).astype(BF16)
    for n, w in enumerate((w_f, w_b)):
        w32[...] = jnp.zeros(w32.shape, F32)
        for a in range(3):
            if n == 0:
                for b in range(3):
                    for e in range(3):
                        t_s[:, (b * 3 + e) * 32:(b * 3 + e) * 32 + 32] = core[a, b, e].astype(F32)
            else:
                blocks = [core[2 - a, 2 - b, 2 - e] for b in range(3) for e in range(3)]
                t_s[:, 0:288] = mm_nt(eye, jnp.concatenate(blocks, axis=0))
            for yy in range(8):
                lo = 96 if yy == 0 else 0
                hi = 192 if yy == 7 else 288
                at = a * 768 + 96 * (yy - 1) + lo
                w32[yy * 32:yy * 32 + 32, at:at + hi - lo] = t_s[:, lo:hi]
            y32[n, 0, :, a * 96:a * 96 + 96] = t_s[:, 0:96]
            y32[n, 1, :, a * 96:a * 96 + 96] = t_s[:, 192:288]
        w[...] = w32[...].astype(BF16)
    wk_t[...] = spread_t(inf[...])

    for w, xs, acc in ((w_b, xs_g, acc_b), (w_f, xs_r, acc_m)):
        for t in range(4):
            k = jnp.concatenate([xs[:, (a + 2 * t) * 128:(a + 2 * t) * 128 + 256] for a in range(3)], axis=0)
            acc[:, t * 256:t * 256 + 256] = mm(w[...], k)
    pl.semaphore_wait(known.at[1], known_due)
    known_due = greet(known.at[2], [(True, 2, 0), (True, -2, 0), (True, 4, 0)])
    g = jnp.zeros((192, 384), F32)
    for p in range(4):
        k = jnp.concatenate([red[64 * p:64 * p + 128, a * 128:a * 128 + 1024] for a in range(3)], axis=0)
        g = g + mm_nt(xs_g[192 * p:192 * p + 192, 128:1152], k)
    for a in range(3):
        second = pltpu.roll(g[96:192, a * 128:a * 128 + 128], 96, 1)
        own[a] = g[0:96, a * 128:a * 128 + 128] + second

    def halo_copies(field, hx, hy):
        for way in range(8):
            arrive(field, way)
        for side in range(2):
            copies = z_copies(hx[side].astype(F32))
            for yy in range(8):
                for e in range(3):
                    hxs[side, yy * 96 + e * 32:yy * 96 + e * 32 + 32, :] = copies[e][yy * 32:yy * 32 + 32]
            for xp in range(10):
                copies = z_copies(hy[side, :, xp * 128:xp * 128 + 128].astype(F32))
                for e in range(3):
                    hys[side, e * 32:e * 32 + 32, xp * 128:xp * 128 + 128] = copies[e]

    def correct(n, w, acc):
        for side in range(2):
            at = 896 * side
            acc[:, at:at + 128] += mm(w[:, 1536 * side:1536 * side + 768], hxs[side])
            k = jnp.concatenate([hys[side, :, a * 128:a * 128 + 1024] for a in range(3)], axis=0)
            acc[224 * side:224 * side + 32, :] += mm(y32[n, side, :, 0:288].astype(BF16), k)
        return acc[...].astype(BF16)

    halo_copies(0, hx_g, hy_g)
    g_x = []
    for side in range(2):
        lanes = pl.ds(128 + 896 * side, 128)
        g_x.append(sum(mm_nt(hxs[side, 192 * p:192 * p + 192, :], red[64 * p:64 * p + 128, lanes]) for p in range(4)))
    g_y = jnp.zeros((288, 128), F32)
    for side in range(2):
        k = jnp.concatenate([hys[side, :, (2 - a) * 128:(2 - a) * 128 + 1024] for a in range(3)], axis=0)
        row = red[32 + 224 * side:64 + 224 * side, 128:1152]
        none = jnp.zeros_like(row)
        row = jnp.concatenate([none, none, row, none] if side == 0 else [row, none, none, none], axis=0)
        g_y = g_y + mm_nt(k, row)
    for a in range(3):
        total = own[a] + g_y[a * 96:a * 96 + 96]
        if a != 1:
            gxx = g_x[0] if a == 2 else g_x[1]
            total = total + gxx[0:96] + pltpu.roll(gxx[96:192], 96, 1)
        for e in range(3):
            part[:, a * 3 + 2 - e, :] = total[e * 32:e * 32 + 32]

    def wait_all(ref, sem):
        pltpu.make_async_copy(ref, ref, sem).wait()

    def start_y(buf, n):
        for k in range(1, 4):
            pltpu.make_async_remote_copy(
                src_ref=buf.at[my_y], dst_ref=buf.at[my_y], send_sem=ar_sem.at[n], recv_sem=ar_sem.at[n + 1],
                device_id=by_y((my_y + k) % 4), device_id_type=MESH).start()

    def member(k):
        q = k // 2
        there_x, there_z, there_c = (x + n_x // 2 + q // n_z) % n_x, (z + n_z // 2 + q) % n_z, (cr + k) % 2
        return (there_x * n_z + there_z) * 2 + there_c, (there_x * 2 + y_lo, there_z * 4 + y_hi * 2 + there_c)

    myself = 2 * ((n_x // 2) * n_z + n_z // 2)

    def each_member(body):
        lax.fori_loop(0, myself, body, 0)
        lax.fori_loop(myself + 1, group, body, 0)

    def start_rs(k, c):
        j, who = member(k)
        slot = jnp.where(k < myself, k, k - 1)
        pltpu.make_async_remote_copy(
            src_ref=part.at[pl.ds(j * per, per)], dst_ref=rs_recv.at[slot], send_sem=ar_sem.at[0], recv_sem=ar_sem.at[1],
            device_id=who, device_id_type=MESH).start()
        return c

    def start_ag(k, c):
        pltpu.make_async_remote_copy(
            src_ref=fin.at[pl.ds(me * per, per)], dst_ref=fin.at[pl.ds(me * per, per)], send_sem=ar_sem.at[4], recv_sem=ar_sem.at[5],
            device_id=member(k)[1], device_id_type=MESH).start()
        return c

    other = (gx, gy + 1 - 2 * cr)
    mine, theirs = pl.ds(pl.multiple_of(cr * HALF, HALF), HALF), pl.ds(pl.multiple_of((1 - cr) * HALF, HALF), HALF)
    plane = n_x * n_z
    at = x * n_z + z
    results = (gin, gout)

    def to_core(n):
        return pltpu.make_async_remote_copy(
            src_ref=part2.at[n, theirs], dst_ref=c_recv.at[n], send_sem=f_sem.at[n, 0], recv_sem=f_sem.at[n, 1],
            device_id=other, device_id_type=MESH)

    def over_xz(n):
        to_core(n).wait_recv()
        xz_recv[n, at] = part2[n, mine] + c_recv[n]

        def start_xz(k, c):
            there_x, there_z = (x + n_x // 2 + k // n_z) % n_x, (z + n_z // 2 + k) % n_z
            pltpu.make_async_remote_copy(
                src_ref=xz_recv.at[n, at], dst_ref=xz_recv.at[n, at], send_sem=f_sem.at[n, 2], recv_sem=f_sem.at[n, 3],
                device_id=(there_x * 2 + y_lo, there_z * 4 + y_hi * 2 + cr), device_id_type=MESH).start()
            return c

        lax.fori_loop(0, myself // 2, start_xz, 0)
        lax.fori_loop(myself // 2 + 1, plane, start_xz, 0)

    def over_y(n):
        wait_all(xz_recv.at[n, pl.ds(0, plane - 1)], f_sem.at[n, 3])
        y2_recv[n, my_y] = jnp.sum(xz_recv[n], axis=0)
        start_y(y2_recv.at[n], 6 + 2 * n)

    def swap(n):
        return pltpu.make_async_remote_copy(
            src_ref=results[n].at[mine], dst_ref=results[n].at[mine], send_sem=f_sem.at[n, 4], recv_sem=f_sem.at[n, 5],
            device_id=other, device_id_type=MESH)

    def back(n):
        wait_all(y2_recv.at[n, pl.ds(0, 3)], ar_sem.at[7 + 2 * n])
        results[n][mine] = jnp.sum(y2_recv[n], axis=0)
        swap(n).start()

    gr = correct(1, w_b, acc_b)
    part[:, 9, :] = fold(mm_nt(a2[...], gr))
    pl.semaphore_wait(known.at[2], known_due)
    each_member(start_rs)
    for t in range(4):
        r = mm(wk_t[...], gr[:, t * 256:t * 256 + 256])
        for side in range(2):
            gact_v[:, 2 * t + side] = r[:, side * 128:side * 128 + 128].reshape(128, 8, 128).astype(BF16)

    halo_copies(1, hx_r, hy_r)
    mixed = correct(0, w_f, acc_m)
    part2[1] = fold(mm_nt(c2[...], mixed))
    to_core(1).start()

    wait_all(rs_recv, ar_sem.at[1])
    y_recv[my_y] = part[pl.ds(me * per, per)] + jnp.sum(rs_recv[...], axis=0)
    start_y(y_recv, 2)
    over_xz(1)
    wait_all(y_recv.at[pl.ds(0, 3)], ar_sem.at[3])
    fin[pl.ds(me * per, per)] = jnp.sum(y_recv[...], axis=0)
    each_member(start_ag)
    over_y(1)
    back(1)
    wait_all(rs_recv, ar_sem.at[5])
    for a in range(3):
        for e in range(3):
            v = fin[:, a * 3 + e, :]
            for b in range(3):
                gcore[a, b, e] = v[:, b * 32:b * 32 + 32]
    wait_all(rs_recv, ar_sem.at[0])
    wait_all(y_recv.at[pl.ds(0, 3)], ar_sem.at[2])
    wait_all(rs_recv, ar_sem.at[4])
    gin[...] = fin[:, 9, :]
    for n in range(1, 2):
        swap(n).wait_recv()
        to_core(n).wait_send()
        wait_all(xz_recv.at[n, pl.ds(0, plane - 1)], f_sem.at[n, 2])
        wait_all(y2_recv.at[n, pl.ds(0, 3)], ar_sem.at[6 + 2 * n])
        swap(n).wait_send()
    for field in range(2):
        for way in range(8):
            sent(field, way)


def finish(*refs):
    copies = [pltpu.make_async_copy(refs[n], refs[n + 4], refs[8].at[n]) for n in range(4)]
    for c in copies:
        c.start()
    for c in copies:
        c.wait()


def shards(dims, activation, cotangent, in_factor, core, out_factor):
    n_gx, n_gy = dims
    group = n_gx * n_gy // 4
    per = R // group
    vm = pl.BlockSpec(memory_space=pltpu.VMEM)
    hbm = pl.BlockSpec(memory_space=pl.ANY)
    held = pl.pallas_call(
        functools.partial(kernel, dims),
        out_shape=(
            pltpu.VMEM(activation.shape, BF16),
            pltpu.VMEM((3, 3, 3, R, R), F32),
            pltpu.VMEM((R, 128), F32),
            pltpu.VMEM((R, 128), F32),
        ),
        in_specs=[hbm, hbm, vm, vm, vm],
        out_specs=(vm, vm, vm, vm),
        scratch_shapes=[
            pltpu.VMEM((128, 8, 8, 128), BF16),
            pltpu.VMEM((128, 8, 8, 128), BF16),
            pltpu.VMEM((1024, 1024), BF16),
            pltpu.VMEM((1024, 1024), BF16),
            pltpu.VMEM((768, 1280), BF16),
            pltpu.VMEM((768, 1280), BF16),
            pltpu.VMEM((320, 1280), BF16),
            pltpu.VMEM((256, 1024), BF16),
            pltpu.VMEM((2, 256, 128), BF16),
            pltpu.VMEM((2, 256, 128), BF16),
            pltpu.VMEM((2, 32, 1280), BF16),
            pltpu.VMEM((2, 32, 1280), BF16),
            pltpu.VMEM((2, 768, 128), BF16),
            pltpu.VMEM((2, 96, 1280), BF16),
            pltpu.VMEM((32, 384), F32),
            pltpu.VMEM((256, 2304), F32),
            pltpu.VMEM((256, 2304), BF16),
            pltpu.VMEM((256, 2304), BF16),
            pltpu.VMEM((2, 2, 32, 384), F32),
            pltpu.VMEM((256, 1024), BF16),
            pltpu.VMEM((256, 1024), BF16),
            pltpu.VMEM((1024, 256), BF16),
            pltpu.VMEM((256, 1024), F32),
            pltpu.VMEM((256, 1024), F32),
            pltpu.VMEM((3, 96, 128), F32),
            pltpu.VMEM((R, ROWS, 128), F32),
            pltpu.VMEM((group - 1, per, ROWS, 128), F32),
            pltpu.VMEM((4, per, ROWS, 128), F32),
            pltpu.VMEM((R, ROWS, 128), F32),
            pltpu.VMEM((2, R, 128), F32),
            pltpu.VMEM((2, HALF, 128), F32),
            pltpu.VMEM((2, group // 2, HALF, 128), F32),
            pltpu.VMEM((2, 4, HALF, 128), F32),
            pltpu.SemaphoreType.DMA((2, 3)),
            pltpu.SemaphoreType.DMA((2, 8)),
            pltpu.SemaphoreType.DMA((2, 8)),
            pltpu.SemaphoreType.DMA((10,)),
            pltpu.SemaphoreType.DMA((2, 6)),
            pltpu.SemaphoreType.REGULAR((3,)),
        ],
        compiler_params=pltpu.CompilerParams(collective_id=0, has_side_effects=True, vmem_limit_bytes=60 * 1024 * 1024),
    )(activation, cotangent, in_factor.T, core, out_factor.T)
    gact, gcore, gin, gout = pl.pallas_call(
        finish,
        out_shape=(
            jax.ShapeDtypeStruct(activation.shape, BF16),
            jax.ShapeDtypeStruct((3, 3, 3, R, R), F32),
            jax.ShapeDtypeStruct((R, 128), F32),
            jax.ShapeDtypeStruct((R, 128), F32),
        ),
        in_specs=[vm] * 4,
        out_specs=(hbm,) * 4,
        scratch_shapes=[pltpu.SemaphoreType.DMA((4,))],
        compiler_params=pltpu.CompilerParams(vmem_limit_bytes=24 * 1024 * 1024),
    )(*held)
    return gact, gin.T, gcore, gout.T


def solution(mesh):
    dims = (mesh.shape["gx"], mesh.shape["gy"])
    placed = (P(None, "gx", "gy", None), P(None, "gx", "gy", None), P(), P(), P())
    return jax.shard_map(
        functools.partial(shards, dims),
        mesh=mesh,
        in_specs=placed,
        out_specs=(P(None, "gx", "gy", None), P(), P(), P()),
        check_vma=False,
    )
```

```python
import functools

import jax
import jax.numpy as jnp
from jax import lax
from jax.experimental import pallas as pl
from jax.experimental.pallas import tpu as pltpu
from jax.sharding import PartitionSpec as P

MESH = pl.DeviceIdType.MESH
F32 = jnp.float32
BF16 = jnp.bfloat16
WAYS = ((1, 0), (-1, 0), (0, 1), (0, -1), (1, 1), (1, -1), (-1, 1), (-1, -1))
R = 32
ROWS = 10
HALF = R // 2


def mm(a, b):
    return lax.dot_general(a, b, (((1,), (0,)), ((), ())), preferred_element_type=F32)


def mm_nt(a, b):
    return lax.dot_general(a, b, (((1,), (1,)), ((), ())), preferred_element_type=F32)


def iota(shape, dim):
    return lax.broadcasted_iota(jnp.int32, shape, dim)


def z_copies(v):
    lane = iota(v.shape, 1)
    less = jnp.where(lane == 0, 0.0, pltpu.roll(v, 1, 1))
    more = jnp.where(lane == 127, 0.0, pltpu.roll(v, 127, 1))
    return less.astype(BF16), v.astype(BF16), more.astype(BF16)


def spread(factor_t):
    repeat = (iota((8 * R, R), 0) % R == iota((8 * R, R), 1)).astype(BF16)
    rows = mm(repeat, factor_t).astype(BF16)
    widen = (iota((128, 1024), 1) // 8 == iota((128, 1024), 0)).astype(BF16)
    wide = mm(rows, widen)
    keep = iota((8 * R, 1024), 1) % 8 == iota((8 * R, 1024), 0) // R
    return jnp.where(keep, wide, 0.0).astype(BF16)


def spread_t(factor_t):
    lift = (iota((1024, 128), 0) // 8 == iota((1024, 128), 1)).astype(BF16)
    repeat = (iota((8 * R, R), 0) % R == iota((8 * R, R), 1)).astype(BF16)
    rows = mm(repeat, factor_t).astype(BF16)
    tall = mm_nt(lift, rows)
    keep = iota((1024, 8 * R), 0) % 8 == iota((1024, 8 * R), 1) // R
    return jnp.where(keep, tall, 0.0).astype(BF16)


def fold(g):
    keep = iota(g.shape, 0) % 8 == iota(g.shape, 1) // R
    g = jnp.where(keep, g, 0.0)
    g = g[:, :128] + g[:, 128:]
    g = jnp.sum(g.reshape(128, 8, 128), axis=1)
    g = g + pltpu.roll(g, 64, 1)
    g = g + pltpu.roll(g, 32, 1)
    return jnp.transpose(g)[:R]


def kernel(dims, act, cot, inf, core, outf, gact_v, gcore, gin, gout,
           act_v, cot_v, a2, c2, xs_r, xs_g, red, gmu, hx_r, hx_g, hy_r, hy_g, hxs, hys,
           t_s, w32, w_f, w_b, y32, wk_i, wk_o, wk_t, acc_m, acc_b, own, part, rs_recv, y_recv, fin, part2, c_recv, xz_recv, y2_recv,
           in_sem, send_sem, recv_sem, ar_sem, f_sem, known):
    n_gx, n_gy = dims
    n_x, n_z = n_gx // 2, n_gy // 4
    group = n_x * n_z * 2
    per = R // group
    gx, gy = lax.axis_index("gx"), lax.axis_index("gy")
    x, y_lo = gx // 2, gx % 2
    z, y_hi, cr = gy // 4, (gy // 2) % 2, gy % 2
    me = (x * n_z + z) * 2 + cr
    my_y = y_hi * 2 + y_lo

    def by_y(j):
        return x * 2 + j % 2, z * 4 + (j // 2) * 2 + cr

    pairs = ((0, 7), (1, 2), (3, 4), (5, 6))
    loads = []
    for n, (src, dst) in enumerate(((cot, cot_v), (act, act_v))):
        mine = []
        for k, xx in enumerate((pl.ds(0, 1), pl.ds(7, 1), pl.ds(1, 6))):
            c = pltpu.make_async_copy(src.at[:, xx], dst.at[:, xx], in_sem.at[n, k])
            c.start()
            mine.append(c)
        loads.append(mine)

    for ref in (hx_r, hx_g, hy_r, hy_g):
        ref[...] = jnp.zeros(ref.shape, BF16)
    barrier = pltpu.get_barrier_semaphore()
    flip = 1 - 2 * cr
    has_up, has_down = z < n_z - 1, z > 0
    first, last = gy == 0, gy == n_gy - 1

    def greet(sem, partners):
        due = 0
        for there, dx, dy in partners:
            who = ((gx + dx + n_gx) % n_gx, gy + dy)
            if there is True:
                pl.semaphore_signal(sem, inc=1, device_id=who, device_id_type=MESH)
                due = due + 1
            else:

                @pl.when(there)
                def _():
                    pl.semaphore_signal(sem, inc=1, device_id=who, device_id_type=MESH)

                due = due + there.astype(jnp.int32)
        return due

    side_l, side_h = 1 - 2 * y_lo, 2 - 4 * y_hi
    up, down = jnp.logical_not(last), jnp.logical_not(first)
    near = [(True if dy == 0 else up if dy > 0 else down, dx, dy) for dx, dy in WAYS]
    near += [(True, dx, dy) for dx in (2, -2) for dy in (0, flip)]
    near += [(has_up, 0, 4), (has_up, 0, 4 + flip), (has_down, 0, -4), (has_down, 0, -4 + flip)]
    near += [(True, dx, dy + dc) for dx, dy in ((side_l, 0), (0, side_h), (side_l, side_h)) for dc in (0, flip)]
    near_due = greet(barrier, near)

    wk_o[...] = spread(outf[...])
    for ref in (xs_r, red):
        ref[:, 0:128] = jnp.zeros((ref.shape[0], 128), BF16)
        ref[:, 1152:1280] = jnp.zeros((ref.shape[0], 128), BF16)
    xs_g[:, 0:128] = jnp.zeros((768, 128), BF16)
    xs_g[:, 1152:1280] = jnp.zeros((768, 128), BF16)
    red[0:32, 128:1152] = jnp.zeros((32, 1024), BF16)
    red[288:320, 128:1152] = jnp.zeros((32, 1024), BF16)

    def inside(gxx, gyy):
        return (gxx >= 0) & (gxx < n_gx) & (gyy >= 0) & (gyy < n_gy)

    def send_copy(field, way):
        dx, dy = WAYS[way]
        src, row0, lane0, hx, hy = (gmu, 0, 0, hx_g, hy_g) if field == 0 else (red, 32, 128, hx_r, hy_r)
        edge_x = lane0 + (896 if dx > 0 else 0)
        edge_y = row0 + (224 if dy > 0 else 0)
        if dy == 0:
            s = src.at[pl.ds(row0, 256), pl.ds(edge_x, 128)]
            d = hx.at[0 if dx > 0 else 1]
        elif dx == 0:
            s = src.at[pl.ds(edge_y, 32), pl.ds(lane0, 1024)]
            d = hy.at[0 if dy > 0 else 1, :, pl.ds(128, 1024)]
        else:
            s = src.at[pl.ds(edge_y, 32), pl.ds(edge_x, 128)]
            d = hy.at[0 if dy > 0 else 1, :, pl.ds(0 if dx > 0 else 1152, 128)]
        return pltpu.make_async_remote_copy(
            src_ref=s, dst_ref=d, send_sem=send_sem.at[field, way], recv_sem=recv_sem.at[field, way],
            device_id=((gx + dx + n_gx) % n_gx, (gy + dy + n_gy) % n_gy), device_id_type=MESH)

    def send(field, way):
        dx, dy = WAYS[way]

        @pl.when(inside(gx + dx, gy + dy))
        def _():
            send_copy(field, way).start()

    def arrive(field, way):
        dx, dy = WAYS[way]

        @pl.when(inside(gx - dx, gy - dy))
        def _():
            send_copy(field, way).wait_recv()

    def sent(field, way):
        dx, dy = WAYS[way]

        @pl.when(inside(gx + dx, gy + dy))
        def _():
            send_copy(field, way).wait_send()

    for field, (raw, flat, wk, xs) in enumerate(((cot_v, c2, wk_o, xs_g), (act_v, a2, wk_i, xs_r))):
        if field == 1:
            wk_i[...] = spread(inf[...])
        for n, p in enumerate(pairs):
            for c in loads[field][0:2] if n == 0 else loads[field][2:3] if n == 1 else ():
                c.wait()
            for xx in p:
                flat[:, xx * 128:xx * 128 + 128] = raw[:, xx].astype(F32).reshape(1024, 128).astype(BF16)
            both = jnp.concatenate([flat[:, xx * 128:xx * 128 + 128] for xx in p], axis=1)
            r = mm(wk[...], both)
            for side, xx in enumerate(p):
                v = r[:, side * 128:side * 128 + 128].astype(BF16).astype(F32)
                copies = z_copies(v)
                if field == 0:
                    gmu[:, xx * 128:xx * 128 + 128] = copies[1]
                else:
                    red[32:288, xx * 128 + 128:xx * 128 + 256] = copies[1]
                for yy in range(8):
                    for e in range(3):
                        xs[yy * 96 + e * 32:yy * 96 + e * 32 + 32, xx * 128 + 128:xx * 128 + 256] = copies[e][yy * 32:yy * 32 + 32]
            if n == 0:
                if field == 0:
                    pl.semaphore_wait(barrier, near_due)
                    known_due = greet(known.at[0], [(True, 2, 0), (True, -2, 0), (has_up, 0, 4), (has_down, 0, -4)])
                send(field, 0)
                send(field, 1)
        for way in range(2, 8):
            send(field, way)

    pl.semaphore_wait(known.at[0], known_due)
    known_due = greet(known.at[1], [(z < n_z - 2, 0, 8), (z > 1, 0, -8)])

    eye = (iota((R, R), 0) == iota((R, R), 1)).astype(BF16)
    for n, w in enumerate((w_f, w_b)):
        w32[...] = jnp.zeros(w32.shape, F32)
        for a in range(3):
            if n == 0:
                for b in range(3):
                    for e in range(3):
                        t_s[:, (b * 3 + e) * 32:(b * 3 + e) * 32 + 32] = core[a, b, e].astype(F32)
            else:
                blocks = [core[2 - a, 2 - b, 2 - e] for b in range(3) for e in range(3)]
                t_s[:, 0:288] = mm_nt(eye, jnp.concatenate(blocks, axis=0))
            for yy in range(8):
                lo = 96 if yy == 0 else 0
                hi = 192 if yy == 7 else 288
                at = a * 768 + 96 * (yy - 1) + lo
                w32[yy * 32:yy * 32 + 32, at:at + hi - lo] = t_s[:, lo:hi]
            y32[n, 0, :, a * 96:a * 96 + 96] = t_s[:, 0:96]
            y32[n, 1, :, a * 96:a * 96 + 96] = t_s[:, 192:288]
        w[...] = w32[...].astype(BF16)
    wk_t[...] = spread_t(inf[...])

    for w, xs, acc in ((w_b, xs_g, acc_b), (w_f, xs_r, acc_m)):
        for t in range(4):
            k = jnp.concatenate([xs[:, (a + 2 * t) * 128:(a + 2 * t) * 128 + 256] for a in range(3)], axis=0)
            acc[:, t * 256:t * 256 + 256] = mm(w[...], k)
    pl.semaphore_wait(known.at[1], known_due)
    known_due = greet(known.at[2], [(True, 2, 0), (True, -2, 0), (True, 4, 0)])
    g = jnp.zeros((192, 384), F32)
    for p in range(4):
        k = jnp.concatenate([red[64 * p:64 * p + 128, a * 128:a * 128 + 1024] for a in range(3)], axis=0)
        g = g + mm_nt(xs_g[192 * p:192 * p + 192, 128:1152], k)
    for a in range(3):
        second = pltpu.roll(g[96:192, a * 128:a * 128 + 128], 96, 1)
        own[a] = g[0:96, a * 128:a * 128 + 128] + second

    def halo_copies(field, hx, hy):
        for way in range(8):
            arrive(field, way)
        for side in range(2):
            copies = z_copies(hx[side].astype(F32))
            for yy in range(8):
                for e in range(3):
                    hxs[side, yy * 96 + e * 32:yy * 96 + e * 32 + 32, :] = copies[e][yy * 32:yy * 32 + 32]
            for xp in range(10):
                copies = z_copies(hy[side, :, xp * 128:xp * 128 + 128].astype(F32))
                for e in range(3):
                    hys[side, e * 32:e * 32 + 32, xp * 128:xp * 128 + 128] = copies[e]

    def correct(n, w, acc):
        for side in range(2):
            at = 896 * side
            acc[:, at:at + 128] += mm(w[:, 1536 * side:1536 * side + 768], hxs[side])
            k = jnp.concatenate([hys[side, :, a * 128:a * 128 + 1024] for a in range(3)], axis=0)
            acc[224 * side:224 * side + 32, :] += mm(y32[n, side, :, 0:288].astype(BF16), k)
        return acc[...].astype(BF16)

    halo_copies(0, hx_g, hy_g)
    g_x = []
    for side in range(2):
        lanes = pl.ds(128 + 896 * side, 128)
        g_x.append(sum(mm_nt(hxs[side, 192 * p:192 * p + 192, :], red[64 * p:64 * p + 128, lanes]) for p in range(4)))
    g_y = jnp.zeros((288, 128), F32)
    for side in range(2):
        k = jnp.concatenate([hys[side, :, (2 - a) * 128:(2 - a) * 128 + 1024] for a in range(3)], axis=0)
        row = red[32 + 224 * side:64 + 224 * side, 128:1152]
        none = jnp.zeros_like(row)
        row = jnp.concatenate([none, none, row, none] if side == 0 else [row, none, none, none], axis=0)
        g_y = g_y + mm_nt(k, row)
    for a in range(3):
        total = own[a] + g_y[a * 96:a * 96 + 96]
        if a != 1:
            gxx = g_x[0] if a == 2 else g_x[1]
            total = total + gxx[0:96] + pltpu.roll(gxx[96:192], 96, 1)
        for e in range(3):
            part[:, a * 3 + 2 - e, :] = total[e * 32:e * 32 + 32]

    def wait_all(ref, sem):
        pltpu.make_async_copy(ref, ref, sem).wait()

    def start_y(buf, n):
        for k in range(1, 4):
            pltpu.make_async_remote_copy(
                src_ref=buf.at[my_y], dst_ref=buf.at[my_y], send_sem=ar_sem.at[n], recv_sem=ar_sem.at[n + 1],
                device_id=by_y((my_y + k) % 4), device_id_type=MESH).start()

    def member(k):
        q = k // 2
        there_x, there_z, there_c = (x + n_x // 2 + q // n_z) % n_x, (z + n_z // 2 + q) % n_z, (cr + k) % 2
        return (there_x * n_z + there_z) * 2 + there_c, (there_x * 2 + y_lo, there_z * 4 + y_hi * 2 + there_c)

    myself = 2 * ((n_x // 2) * n_z + n_z // 2)

    def each_member(body):
        lax.fori_loop(0, myself, body, 0)
        lax.fori_loop(myself + 1, group, body, 0)

    def start_rs(k, c):
        j, who = member(k)
        slot = jnp.where(k < myself, k, k - 1)
        pltpu.make_async_remote_copy(
            src_ref=part.at[pl.ds(j * per, per)], dst_ref=rs_recv.at[slot], send_sem=ar_sem.at[0], recv_sem=ar_sem.at[1],
            device_id=who, device_id_type=MESH).start()
        return c

    def start_ag(k, c):
        pltpu.make_async_remote_copy(
            src_ref=fin.at[pl.ds(me * per, per)], dst_ref=fin.at[pl.ds(me * per, per)], send_sem=ar_sem.at[4], recv_sem=ar_sem.at[5],
            device_id=member(k)[1], device_id_type=MESH).start()
        return c

    other = (gx, gy + 1 - 2 * cr)
    mine, theirs = pl.ds(pl.multiple_of(cr * HALF, HALF), HALF), pl.ds(pl.multiple_of((1 - cr) * HALF, HALF), HALF)
    plane = n_x * n_z
    at = x * n_z + z
    results = (gin, gout)

    def to_core(n):
        return pltpu.make_async_remote_copy(
            src_ref=part2.at[n, theirs], dst_ref=c_recv.at[n], send_sem=f_sem.at[n, 0], recv_sem=f_sem.at[n, 1],
            device_id=other, device_id_type=MESH)

    def over_xz(n):
        to_core(n).wait_recv()
        xz_recv[n, at] = part2[n, mine] + c_recv[n]

        def start_xz(k, c):
            there_x, there_z = (x + n_x // 2 + k // n_z) % n_x, (z + n_z // 2 + k) % n_z
            pltpu.make_async_remote_copy(
                src_ref=xz_recv.at[n, at], dst_ref=xz_recv.at[n, at], send_sem=f_sem.at[n, 2], recv_sem=f_sem.at[n, 3],
                device_id=(there_x * 2 + y_lo, there_z * 4 + y_hi * 2 + cr), device_id_type=MESH).start()
            return c

        lax.fori_loop(0, myself // 2, start_xz, 0)
        lax.fori_loop(myself // 2 + 1, plane, start_xz, 0)

    def over_y(n):
        wait_all(xz_recv.at[n, pl.ds(0, plane - 1)], f_sem.at[n, 3])
        y2_recv[n, my_y * 2 + cr] = jnp.sum(xz_recv[n], axis=0)
        for k in range(1, 8):
            to_y = (my_y + k // 2) % 4
            who = (x * 2 + to_y % 2, z * 4 + (to_y // 2) * 2 + (cr + k) % 2)
            pltpu.make_async_remote_copy(
                src_ref=y2_recv.at[n, my_y * 2 + cr], dst_ref=y2_recv.at[n, my_y * 2 + cr],
                send_sem=f_sem.at[n, 4], recv_sem=f_sem.at[n, 5], device_id=who, device_id_type=MESH).start()

    def back(n):
        wait_all(y2_recv.at[n, pl.ds(0, 7)], f_sem.at[n, 5])
        halves = [(y2_recv[n, c] + y2_recv[n, 2 + c]) + (y2_recv[n, 4 + c] + y2_recv[n, 6 + c]) for c in range(2)]
        results[n][...] = jnp.concatenate(halves, axis=0)

    gr = correct(1, w_b, acc_b)
    part[:, 9, :] = fold(mm_nt(a2[...], gr))
    pl.semaphore_wait(known.at[2], known_due)
    each_member(start_rs)

    halo_copies(1, hx_r, hy_r)
    mixed = correct(0, w_f, acc_m)
    part2[1] = fold(mm_nt(c2[...], mixed))
    to_core(1).start()
    for t in range(4):
        r = mm(wk_t[...], gr[:, t * 256:t * 256 + 256])
        for side in range(2):
            gact_v[:, 2 * t + side] = r[:, side * 128:side * 128 + 128].reshape(128, 8, 128).astype(BF16)
    over_xz(1)

    wait_all(rs_recv, ar_sem.at[1])
    y_recv[my_y] = part[pl.ds(me * per, per)] + jnp.sum(rs_recv[...], axis=0)
    start_y(y_recv, 2)
    wait_all(y_recv.at[pl.ds(0, 3)], ar_sem.at[3])
    fin[pl.ds(me * per, per)] = jnp.sum(y_recv[...], axis=0)
    each_member(start_ag)
    over_y(1)
    back(1)
    wait_all(rs_recv, ar_sem.at[5])
    for a in range(3):
        for e in range(3):
            v = fin[:, a * 3 + e, :]
            for b in range(3):
                gcore[a, b, e] = v[:, b * 32:b * 32 + 32]
    wait_all(rs_recv, ar_sem.at[0])
    wait_all(y_recv.at[pl.ds(0, 3)], ar_sem.at[2])
    wait_all(rs_recv, ar_sem.at[4])
    gin[...] = fin[:, 9, :]
    for n in range(1, 2):
        to_core(n).wait_send()
        wait_all(xz_recv.at[n, pl.ds(0, plane - 1)], f_sem.at[n, 2])
        wait_all(y2_recv.at[n, pl.ds(0, 7)], f_sem.at[n, 4])
    for field in range(2):
        for way in range(8):
            sent(field, way)


def finish(*refs):
    copies = [pltpu.make_async_copy(refs[n], refs[n + 4], refs[8].at[n]) for n in range(4)]
    for c in copies:
        c.start()
    for c in copies:
        c.wait()


def shards(dims, activation, cotangent, in_factor, core, out_factor):
    n_gx, n_gy = dims
    group = n_gx * n_gy // 4
    per = R // group
    vm = pl.BlockSpec(memory_space=pltpu.VMEM)
    hbm = pl.BlockSpec(memory_space=pl.ANY)
    held = pl.pallas_call(
        functools.partial(kernel, dims),
        out_shape=(
            pltpu.VMEM(activation.shape, BF16),
            pltpu.VMEM((3, 3, 3, R, R), F32),
            pltpu.VMEM((R, 128), F32),
            pltpu.VMEM((R, 128), F32),
        ),
        in_specs=[hbm, hbm, vm, vm, vm],
        out_specs=(vm, vm, vm, vm),
        scratch_shapes=[
            pltpu.VMEM((128, 8, 8, 128), BF16),
            pltpu.VMEM((128, 8, 8, 128), BF16),
            pltpu.VMEM((1024, 1024), BF16),
            pltpu.VMEM((1024, 1024), BF16),
            pltpu.VMEM((768, 1280), BF16),
            pltpu.VMEM((768, 1280), BF16),
            pltpu.VMEM((320, 1280), BF16),
            pltpu.VMEM((256, 1024), BF16),
            pltpu.VMEM((2, 256, 128), BF16),
            pltpu.VMEM((2, 256, 128), BF16),
            pltpu.VMEM((2, 32, 1280), BF16),
            pltpu.VMEM((2, 32, 1280), BF16),
            pltpu.VMEM((2, 768, 128), BF16),
            pltpu.VMEM((2, 96, 1280), BF16),
            pltpu.VMEM((32, 384), F32),
            pltpu.VMEM((256, 2304), F32),
            pltpu.VMEM((256, 2304), BF16),
            pltpu.VMEM((256, 2304), BF16),
            pltpu.VMEM((2, 2, 32, 384), F32),
            pltpu.VMEM((256, 1024), BF16),
            pltpu.VMEM((256, 1024), BF16),
            pltpu.VMEM((1024, 256), BF16),
            pltpu.VMEM((256, 1024), F32),
            pltpu.VMEM((256, 1024), F32),
            pltpu.VMEM((3, 96, 128), F32),
            pltpu.VMEM((R, ROWS, 128), F32),
            pltpu.VMEM((group - 1, per, ROWS, 128), F32),
            pltpu.VMEM((4, per, ROWS, 128), F32),
            pltpu.VMEM((R, ROWS, 128), F32),
            pltpu.VMEM((2, R, 128), F32),
            pltpu.VMEM((2, HALF, 128), F32),
            pltpu.VMEM((2, group // 2, HALF, 128), F32),
            pltpu.VMEM((2, 8, HALF, 128), F32),
            pltpu.SemaphoreType.DMA((2, 3)),
            pltpu.SemaphoreType.DMA((2, 8)),
            pltpu.SemaphoreType.DMA((2, 8)),
            pltpu.SemaphoreType.DMA((10,)),
            pltpu.SemaphoreType.DMA((2, 6)),
            pltpu.SemaphoreType.REGULAR((3,)),
        ],
        compiler_params=pltpu.CompilerParams(collective_id=0, has_side_effects=True, vmem_limit_bytes=60 * 1024 * 1024),
    )(activation, cotangent, in_factor.T, core, out_factor.T)
    gact, gcore, gin, gout = pl.pallas_call(
        finish,
        out_shape=(
            jax.ShapeDtypeStruct(activation.shape, BF16),
            jax.ShapeDtypeStruct((3, 3, 3, R, R), F32),
            jax.ShapeDtypeStruct((R, 128), F32),
            jax.ShapeDtypeStruct((R, 128), F32),
        ),
        in_specs=[vm] * 4,
        out_specs=(hbm,) * 4,
        scratch_shapes=[pltpu.SemaphoreType.DMA((4,))],
        compiler_params=pltpu.CompilerParams(vmem_limit_bytes=24 * 1024 * 1024),
    )(*held)
    return gact, gin.T, gcore, gout.T


def solution(mesh):
    dims = (mesh.shape["gx"], mesh.shape["gy"])
    placed = (P(None, "gx", "gy", None), P(None, "gx", "gy", None), P(), P(), P())
    return jax.shard_map(
        functools.partial(shards, dims),
        mesh=mesh,
        in_specs=placed,
        out_specs=(P(None, "gx", "gy", None), P(), P(), P()),
        check_vma=False,
    )
```

```python
import functools

import jax
import jax.numpy as jnp
from jax import lax
from jax.experimental import pallas as pl
from jax.experimental.pallas import tpu as pltpu
from jax.sharding import PartitionSpec as P

MESH = pl.DeviceIdType.MESH
F32 = jnp.float32
BF16 = jnp.bfloat16
WAYS = ((1, 0), (-1, 0), (0, 1), (0, -1), (1, 1), (1, -1), (-1, 1), (-1, -1))
R = 32
ROWS = 10
HALF = R // 2


def mm(a, b):
    return lax.dot_general(a, b, (((1,), (0,)), ((), ())), preferred_element_type=F32)


def mm_nt(a, b):
    return lax.dot_general(a, b, (((1,), (1,)), ((), ())), preferred_element_type=F32)


def iota(shape, dim):
    return lax.broadcasted_iota(jnp.int32, shape, dim)


def z_copies(v):
    lane = iota(v.shape, 1)
    less = jnp.where(lane == 0, jnp.zeros_like(v), pltpu.roll(v, 1, 1))
    more = jnp.where(lane == 127, jnp.zeros_like(v), pltpu.roll(v, 127, 1))
    return less, v, more


def spread(factor_t):
    repeat = (iota((8 * R, R), 0) % R == iota((8 * R, R), 1)).astype(BF16)
    rows = mm(repeat, factor_t).astype(BF16)
    widen = (iota((128, 1024), 1) // 8 == iota((128, 1024), 0)).astype(BF16)
    wide = mm(rows, widen)
    keep = iota((8 * R, 1024), 1) % 8 == iota((8 * R, 1024), 0) // R
    return jnp.where(keep, wide, 0.0).astype(BF16)


def spread_t(factor_t):
    lift = (iota((1024, 128), 0) // 8 == iota((1024, 128), 1)).astype(BF16)
    repeat = (iota((8 * R, R), 0) % R == iota((8 * R, R), 1)).astype(BF16)
    rows = mm(repeat, factor_t).astype(BF16)
    tall = mm_nt(lift, rows)
    keep = iota((1024, 8 * R), 0) % 8 == iota((1024, 8 * R), 1) // R
    return jnp.where(keep, tall, 0.0).astype(BF16)


def fold(g):
    keep = iota(g.shape, 0) % 8 == iota(g.shape, 1) // R
    g = jnp.where(keep, g, 0.0)
    g = g[:, :128] + g[:, 128:]
    g = jnp.sum(g.reshape(128, 8, 128), axis=1)
    g = g + pltpu.roll(g, 64, 1)
    g = g + pltpu.roll(g, 32, 1)
    return jnp.transpose(g)[:R]


def kernel(dims, act, cot, inf, core, outf, gact_v, gcore, gin, gout,
           act_v, cot_v, a2, c2, xs_r, xs_g, red, gmu, hx_r, hx_g, hy_r, hy_g, hxs, hys,
           t_s, w32, w_f, w_b, y32, wk_i, wk_o, wk_t, acc_m, acc_b, own, part, rs_recv, y_recv, fin, part2, c_recv, xz_recv, y2_recv,
           in_sem, send_sem, recv_sem, ar_sem, f_sem, known):
    n_gx, n_gy = dims
    n_x, n_z = n_gx // 2, n_gy // 4
    group = n_x * n_z * 2
    per = R // group
    gx, gy = lax.axis_index("gx"), lax.axis_index("gy")
    x, y_lo = gx // 2, gx % 2
    z, y_hi, cr = gy // 4, (gy // 2) % 2, gy % 2
    me = (x * n_z + z) * 2 + cr
    my_y = y_hi * 2 + y_lo

    def by_y(j):
        return x * 2 + j % 2, z * 4 + (j // 2) * 2 + cr

    pairs = ((0, 7), (1, 2), (3, 4), (5, 6))
    loads = []
    for n, (src, dst) in enumerate(((cot, cot_v), (act, act_v))):
        mine = []
        for k, xx in enumerate((pl.ds(0, 1), pl.ds(7, 1), pl.ds(1, 6))):
            c = pltpu.make_async_copy(src.at[:, xx], dst.at[:, xx], in_sem.at[n, k])
            c.start()
            mine.append(c)
        loads.append(mine)

    for ref in (hx_r, hx_g, hy_r, hy_g):
        ref[...] = jnp.zeros(ref.shape, BF16)
    barrier = pltpu.get_barrier_semaphore()
    flip = 1 - 2 * cr
    has_up, has_down = z < n_z - 1, z > 0
    first, last = gy == 0, gy == n_gy - 1

    def greet(sem, partners):
        due = 0
        for there, dx, dy in partners:
            who = ((gx + dx + n_gx) % n_gx, gy + dy)
            if there is True:
                pl.semaphore_signal(sem, inc=1, device_id=who, device_id_type=MESH)
                due = due + 1
            else:

                @pl.when(there)
                def _():
                    pl.semaphore_signal(sem, inc=1, device_id=who, device_id_type=MESH)

                due = due + there.astype(jnp.int32)
        return due

    side_l, side_h = 1 - 2 * y_lo, 2 - 4 * y_hi
    up, down = jnp.logical_not(last), jnp.logical_not(first)
    near = [(True if dy == 0 else up if dy > 0 else down, dx, dy) for dx, dy in WAYS]
    near += [(True, dx, dy) for dx in (2, -2) for dy in (0, flip)]
    near += [(has_up, 0, 4), (has_up, 0, 4 + flip), (has_down, 0, -4), (has_down, 0, -4 + flip)]
    near += [(True, dx, dy + dc) for dx, dy in ((side_l, 0), (0, side_h), (side_l, side_h)) for dc in (0, flip)]
    near_due = greet(barrier, near)

    wk_o[...] = spread(outf[...])
    for ref in (xs_r, red):
        ref[:, 0:128] = jnp.zeros((ref.shape[0], 128), BF16)
        ref[:, 1152:1280] = jnp.zeros((ref.shape[0], 128), BF16)
    xs_g[:, 0:128] = jnp.zeros((768, 128), BF16)
    xs_g[:, 1152:1280] = jnp.zeros((768, 128), BF16)
    red[0:32, 128:1152] = jnp.zeros((32, 1024), BF16)
    red[288:320, 128:1152] = jnp.zeros((32, 1024), BF16)

    def inside(gxx, gyy):
        return (gxx >= 0) & (gxx < n_gx) & (gyy >= 0) & (gyy < n_gy)

    def send_copy(field, way):
        dx, dy = WAYS[way]
        src, row0, lane0, hx, hy = (gmu, 0, 0, hx_g, hy_g) if field == 0 else (red, 32, 128, hx_r, hy_r)
        edge_x = lane0 + (896 if dx > 0 else 0)
        edge_y = row0 + (224 if dy > 0 else 0)
        if dy == 0:
            s = src.at[pl.ds(row0, 256), pl.ds(edge_x, 128)]
            d = hx.at[0 if dx > 0 else 1]
        elif dx == 0:
            s = src.at[pl.ds(edge_y, 32), pl.ds(lane0, 1024)]
            d = hy.at[0 if dy > 0 else 1, :, pl.ds(128, 1024)]
        else:
            s = src.at[pl.ds(edge_y, 32), pl.ds(edge_x, 128)]
            d = hy.at[0 if dy > 0 else 1, :, pl.ds(0 if dx > 0 else 1152, 128)]
        return pltpu.make_async_remote_copy(
            src_ref=s, dst_ref=d, send_sem=send_sem.at[field, way], recv_sem=recv_sem.at[field, way],
            device_id=((gx + dx + n_gx) % n_gx, (gy + dy + n_gy) % n_gy), device_id_type=MESH)

    def send(field, way):
        dx, dy = WAYS[way]

        @pl.when(inside(gx + dx, gy + dy))
        def _():
            send_copy(field, way).start()

    def arrive(field, way):
        dx, dy = WAYS[way]

        @pl.when(inside(gx - dx, gy - dy))
        def _():
            send_copy(field, way).wait_recv()

    def sent(field, way):
        dx, dy = WAYS[way]

        @pl.when(inside(gx + dx, gy + dy))
        def _():
            send_copy(field, way).wait_send()

    for field, (raw, flat, wk, xs) in enumerate(((cot_v, c2, wk_o, xs_g), (act_v, a2, wk_i, xs_r))):
        if field == 1:
            wk_i[...] = spread(inf[...])
        for n, p in enumerate(pairs):
            for c in loads[field][0:2] if n == 0 else loads[field][2:3] if n == 1 else ():
                c.wait()
            for xx in p:
                flat[:, xx * 128:xx * 128 + 128] = raw[:, xx].astype(F32).reshape(1024, 128).astype(BF16)
            both = jnp.concatenate([flat[:, xx * 128:xx * 128 + 128] for xx in p], axis=1)
            r = mm(wk[...], both)
            for side, xx in enumerate(p):
                v = r[:, side * 128:side * 128 + 128].astype(BF16)
                copies = z_copies(v)
                if field == 0:
                    gmu[:, xx * 128:xx * 128 + 128] = copies[1]
                else:
                    red[32:288, xx * 128 + 128:xx * 128 + 256] = copies[1]
                for yy in range(8):
                    for e in range(3):
                        xs[yy * 96 + e * 32:yy * 96 + e * 32 + 32, xx * 128 + 128:xx * 128 + 256] = copies[e][yy * 32:yy * 32 + 32]
            if n == 0:
                if field == 0:
                    pl.semaphore_wait(barrier, near_due)
                    known_due = greet(known.at[0], [(True, 2, 0), (True, -2, 0), (has_up, 0, 4), (has_down, 0, -4)])
                send(field, 0)
                send(field, 1)
        for way in range(2, 8):
            send(field, way)

    pl.semaphore_wait(known.at[0], known_due)
    known_due = greet(known.at[1], [(z < n_z - 2, 0, 8), (z > 1, 0, -8)])

    eye = (iota((R, R), 0) == iota((R, R), 1)).astype(BF16)
    w32[...] = jnp.zeros(w32.shape, F32)
    for n, w in enumerate((w_f, w_b)):
        for a in range(3):
            if n == 0:
                for b in range(3):
                    for e in range(3):
                        t_s[:, (b * 3 + e) * 32:(b * 3 + e) * 32 + 32] = core[a, b, e].astype(F32)
            else:
                blocks = [core[2 - a, 2 - b, 2 - e] for b in range(3) for e in range(3)]
                t_s[:, 0:288] = mm_nt(eye, jnp.concatenate(blocks, axis=0))
            for yy in range(8):
                lo = 96 if yy == 0 else 0
                hi = 192 if yy == 7 else 288
                at = a * 768 + 96 * (yy - 1) + lo
                w32[yy * 32:yy * 32 + 32, at:at + hi - lo] = t_s[:, lo:hi]
            y32[n, 0, :, a * 96:a * 96 + 96] = t_s[:, 0:96]
            y32[n, 1, :, a * 96:a * 96 + 96] = t_s[:, 192:288]
        w[...] = w32[...].astype(BF16)
    wk_t[...] = spread_t(inf[...])

    for w, xs, acc in ((w_b, xs_g, acc_b), (w_f, xs_r, acc_m)):
        for t in range(4):
            k = jnp.concatenate([xs[:, (a + 2 * t) * 128:(a + 2 * t) * 128 + 256] for a in range(3)], axis=0)
            acc[:, t * 256:t * 256 + 256] = mm(w[...], k)
    pl.semaphore_wait(known.at[1], known_due)
    known_due = greet(known.at[2], [(True, 2, 0), (True, -2, 0), (True, 4, 0)])
    g = jnp.zeros((192, 384), F32)
    for p in range(4):
        k = jnp.concatenate([red[64 * p:64 * p + 128, a * 128:a * 128 + 1024] for a in range(3)], axis=0)
        g = g + mm_nt(xs_g[192 * p:192 * p + 192, 128:1152], k)
    for a in range(3):
        second = pltpu.roll(g[96:192, a * 128:a * 128 + 128], 96, 1)
        own[a] = g[0:96, a * 128:a * 128 + 128] + second

    def halo_x(field, hx):
        for way in range(2):
            arrive(field, way)
        for side in range(2):
            copies = z_copies(hx[side])
            for yy in range(8):
                for e in range(3):
                    hxs[side, yy * 96 + e * 32:yy * 96 + e * 32 + 32, :] = copies[e][yy * 32:yy * 32 + 32]

    def halo_y(field, hy):
        for way in range(2, 8):
            arrive(field, way)
        for side in range(2):
            for xp in range(10):
                copies = z_copies(hy[side, :, xp * 128:xp * 128 + 128])
                for e in range(3):
                    hys[side, e * 32:e * 32 + 32, xp * 128:xp * 128 + 128] = copies[e]

    def correct_x(w, acc):
        for side in range(2):
            at = 896 * side
            acc[:, at:at + 128] += mm(w[:, 1536 * side:1536 * side + 768], hxs[side])

    def correct_y(n, acc):
        for side in range(2):
            k = jnp.concatenate([hys[side, :, a * 128:a * 128 + 1024] for a in range(3)], axis=0)
            acc[224 * side:224 * side + 32, :] += mm(y32[n, side, :, 0:288].astype(BF16), k)
        return acc[...].astype(BF16)

    halo_x(0, hx_g)
    correct_x(w_b, acc_b)
    g_x = []
    for side in range(2):
        lanes = pl.ds(128 + 896 * side, 128)
        g_x.append(sum(mm_nt(hxs[side, 192 * p:192 * p + 192, :], red[64 * p:64 * p + 128, lanes]) for p in range(4)))
    halo_y(0, hy_g)
    g_y = jnp.zeros((288, 128), F32)
    for side in range(2):
        k = jnp.concatenate([hys[side, :, (2 - a) * 128:(2 - a) * 128 + 1024] for a in range(3)], axis=0)
        row = red[32 + 224 * side:64 + 224 * side, 128:1152]
        none = jnp.zeros_like(row)
        row = jnp.concatenate([none, none, row, none] if side == 0 else [row, none, none, none], axis=0)
        g_y = g_y + mm_nt(k, row)
    for a in range(3):
        total = own[a] + g_y[a * 96:a * 96 + 96]
        if a != 1:
            gxx = g_x[0] if a == 2 else g_x[1]
            total = total + gxx[0:96] + pltpu.roll(gxx[96:192], 96, 1)
        for e in range(3):
            part[:, a * 3 + 2 - e, :] = total[e * 32:e * 32 + 32]

    def wait_all(ref, sem):
        pltpu.make_async_copy(ref, ref, sem).wait()

    def start_y(buf, n):
        for k in range(1, 4):
            pltpu.make_async_remote_copy(
                src_ref=buf.at[my_y], dst_ref=buf.at[my_y], send_sem=ar_sem.at[n], recv_sem=ar_sem.at[n + 1],
                device_id=by_y((my_y + k) % 4), device_id_type=MESH).start()

    def member(k):
        q = k // 2
        there_x, there_z, there_c = (x + n_x // 2 + q // n_z) % n_x, (z + n_z // 2 + q) % n_z, (cr + k) % 2
        return (there_x * n_z + there_z) * 2 + there_c, (there_x * 2 + y_lo, there_z * 4 + y_hi * 2 + there_c)

    myself = 2 * ((n_x // 2) * n_z + n_z // 2)

    def each_member(body):
        lax.fori_loop(0, myself, body, 0)
        lax.fori_loop(myself + 1, group, body, 0)

    def start_rs(k, c):
        j, who = member(k)
        slot = jnp.where(k < myself, k, k - 1)
        pltpu.make_async_remote_copy(
            src_ref=part.at[pl.ds(j * per, per)], dst_ref=rs_recv.at[slot], send_sem=ar_sem.at[0], recv_sem=ar_sem.at[1],
            device_id=who, device_id_type=MESH).start()
        return c

    def start_ag(k, c):
        pltpu.make_async_remote_copy(
            src_ref=fin.at[pl.ds(me * per, per)], dst_ref=fin.at[pl.ds(me * per, per)], send_sem=ar_sem.at[4], recv_sem=ar_sem.at[5],
            device_id=member(k)[1], device_id_type=MESH).start()
        return c

    other = (gx, gy + 1 - 2 * cr)
    mine, theirs = pl.ds(pl.multiple_of(cr * HALF, HALF), HALF), pl.ds(pl.multiple_of((1 - cr) * HALF, HALF), HALF)
    plane = n_x * n_z
    at = x * n_z + z
    results = (gin, gout)

    def to_core(n):
        return pltpu.make_async_remote_copy(
            src_ref=part2.at[n, theirs], dst_ref=c_recv.at[n], send_sem=f_sem.at[n, 0], recv_sem=f_sem.at[n, 1],
            device_id=other, device_id_type=MESH)

    def over_xz(n):
        to_core(n).wait_recv()
        xz_recv[n, at] = part2[n, mine] + c_recv[n]

        def start_xz(k, c):
            there_x, there_z = (x + n_x // 2 + k // n_z) % n_x, (z + n_z // 2 + k) % n_z
            pltpu.make_async_remote_copy(
                src_ref=xz_recv.at[n, at], dst_ref=xz_recv.at[n, at], send_sem=f_sem.at[n, 2], recv_sem=f_sem.at[n, 3],
                device_id=(there_x * 2 + y_lo, there_z * 4 + y_hi * 2 + cr), device_id_type=MESH).start()
            return c

        lax.fori_loop(0, myself // 2, start_xz, 0)
        lax.fori_loop(myself // 2 + 1, plane, start_xz, 0)

    def over_y(n):
        wait_all(xz_recv.at[n, pl.ds(0, plane - 1)], f_sem.at[n, 3])
        y2_recv[n, my_y * 2 + cr] = jnp.sum(xz_recv[n], axis=0)
        for k in range(1, 8):
            to_y = (my_y + k // 2) % 4
            who = (x * 2 + to_y % 2, z * 4 + (to_y // 2) * 2 + (cr + k) % 2)
            pltpu.make_async_remote_copy(
                src_ref=y2_recv.at[n, my_y * 2 + cr], dst_ref=y2_recv.at[n, my_y * 2 + cr],
                send_sem=f_sem.at[n, 4], recv_sem=f_sem.at[n, 5], device_id=who, device_id_type=MESH).start()

    def back(n):
        wait_all(y2_recv.at[n, pl.ds(0, 7)], f_sem.at[n, 5])
        halves = [(y2_recv[n, c] + y2_recv[n, 2 + c]) + (y2_recv[n, 4 + c] + y2_recv[n, 6 + c]) for c in range(2)]
        results[n][...] = jnp.concatenate(halves, axis=0)

    gr = correct_y(1, acc_b)
    part[:, 9, :] = fold(mm_nt(a2[...], gr))
    pl.semaphore_wait(known.at[2], known_due)
    each_member(start_rs)

    halo_x(1, hx_r)
    correct_x(w_f, acc_m)
    halo_y(1, hy_r)
    mixed = correct_y(0, acc_m)
    part2[1] = fold(mm_nt(c2[...], mixed))
    to_core(1).start()
    for t in range(4):
        r = mm(wk_t[...], gr[:, t * 256:t * 256 + 256])
        for side in range(2):
            gact_v[:, 2 * t + side] = r[:, side * 128:side * 128 + 128].reshape(128, 8, 128).astype(BF16)
    over_xz(1)

    wait_all(rs_recv, ar_sem.at[1])
    y_recv[my_y] = part[pl.ds(me * per, per)] + jnp.sum(rs_recv[...], axis=0)
    start_y(y_recv, 2)
    wait_all(y_recv.at[pl.ds(0, 3)], ar_sem.at[3])
    fin[pl.ds(me * per, per)] = jnp.sum(y_recv[...], axis=0)
    each_member(start_ag)
    over_y(1)
    back(1)
    wait_all(rs_recv, ar_sem.at[5])
    for a in range(3):
        for e in range(3):
            v = fin[:, a * 3 + e, :]
            for b in range(3):
                gcore[a, b, e] = v[:, b * 32:b * 32 + 32]
    wait_all(rs_recv, ar_sem.at[0])
    wait_all(y_recv.at[pl.ds(0, 3)], ar_sem.at[2])
    wait_all(rs_recv, ar_sem.at[4])
    gin[...] = fin[:, 9, :]
    for n in range(1, 2):
        to_core(n).wait_send()
        wait_all(xz_recv.at[n, pl.ds(0, plane - 1)], f_sem.at[n, 2])
        wait_all(y2_recv.at[n, pl.ds(0, 7)], f_sem.at[n, 4])
    for field in range(2):
        for way in range(8):
            sent(field, way)


def finish(*refs):
    copies = [pltpu.make_async_copy(refs[n], refs[n + 4], refs[8].at[n]) for n in range(4)]
    for c in copies:
        c.start()
    for c in copies:
        c.wait()


def shards(dims, activation, cotangent, in_factor, core, out_factor):
    n_gx, n_gy = dims
    group = n_gx * n_gy // 4
    per = R // group
    vm = pl.BlockSpec(memory_space=pltpu.VMEM)
    hbm = pl.BlockSpec(memory_space=pl.ANY)
    held = pl.pallas_call(
        functools.partial(kernel, dims),
        out_shape=(
            pltpu.VMEM(activation.shape, BF16),
            pltpu.VMEM((3, 3, 3, R, R), F32),
            pltpu.VMEM((R, 128), F32),
            pltpu.VMEM((R, 128), F32),
        ),
        in_specs=[hbm, hbm, vm, vm, vm],
        out_specs=(vm, vm, vm, vm),
        scratch_shapes=[
            pltpu.VMEM((128, 8, 8, 128), BF16),
            pltpu.VMEM((128, 8, 8, 128), BF16),
            pltpu.VMEM((1024, 1024), BF16),
            pltpu.VMEM((1024, 1024), BF16),
            pltpu.VMEM((768, 1280), BF16),
            pltpu.VMEM((768, 1280), BF16),
            pltpu.VMEM((320, 1280), BF16),
            pltpu.VMEM((256, 1024), BF16),
            pltpu.VMEM((2, 256, 128), BF16),
            pltpu.VMEM((2, 256, 128), BF16),
            pltpu.VMEM((2, 32, 1280), BF16),
            pltpu.VMEM((2, 32, 1280), BF16),
            pltpu.VMEM((2, 768, 128), BF16),
            pltpu.VMEM((2, 96, 1280), BF16),
            pltpu.VMEM((32, 384), F32),
            pltpu.VMEM((256, 2304), F32),
            pltpu.VMEM((256, 2304), BF16),
            pltpu.VMEM((256, 2304), BF16),
            pltpu.VMEM((2, 2, 32, 384), F32),
            pltpu.VMEM((256, 1024), BF16),
            pltpu.VMEM((256, 1024), BF16),
            pltpu.VMEM((1024, 256), BF16),
            pltpu.VMEM((256, 1024), F32),
            pltpu.VMEM((256, 1024), F32),
            pltpu.VMEM((3, 96, 128), F32),
            pltpu.VMEM((R, ROWS, 128), F32),
            pltpu.VMEM((group - 1, per, ROWS, 128), F32),
            pltpu.VMEM((4, per, ROWS, 128), F32),
            pltpu.VMEM((R, ROWS, 128), F32),
            pltpu.VMEM((2, R, 128), F32),
            pltpu.VMEM((2, HALF, 128), F32),
            pltpu.VMEM((2, group // 2, HALF, 128), F32),
            pltpu.VMEM((2, 8, HALF, 128), F32),
            pltpu.SemaphoreType.DMA((2, 3)),
            pltpu.SemaphoreType.DMA((2, 8)),
            pltpu.SemaphoreType.DMA((2, 8)),
            pltpu.SemaphoreType.DMA((10,)),
            pltpu.SemaphoreType.DMA((2, 6)),
            pltpu.SemaphoreType.REGULAR((3,)),
        ],
        compiler_params=pltpu.CompilerParams(collective_id=0, has_side_effects=True, vmem_limit_bytes=60 * 1024 * 1024),
    )(activation, cotangent, in_factor.T, core, out_factor.T)
    gact, gcore, gin, gout = pl.pallas_call(
        finish,
        out_shape=(
            jax.ShapeDtypeStruct(activation.shape, BF16),
            jax.ShapeDtypeStruct((3, 3, 3, R, R), F32),
            jax.ShapeDtypeStruct((R, 128), F32),
            jax.ShapeDtypeStruct((R, 128), F32),
        ),
        in_specs=[vm] * 4,
        out_specs=(hbm,) * 4,
        scratch_shapes=[pltpu.SemaphoreType.DMA((4,))],
        compiler_params=pltpu.CompilerParams(vmem_limit_bytes=24 * 1024 * 1024),
    )(*held)
    return gact, gin.T, gcore, gout.T


def solution(mesh):
    dims = (mesh.shape["gx"], mesh.shape["gy"])
    placed = (P(None, "gx", "gy", None), P(None, "gx", "gy", None), P(), P(), P())
    return jax.shard_map(
        functools.partial(shards, dims),
        mesh=mesh,
        in_specs=placed,
        out_specs=(P(None, "gx", "gy", None), P(), P(), P()),
        check_vma=False,
    )
```

```python
import functools

import jax
import jax.numpy as jnp
from jax import lax
from jax.experimental import pallas as pl
from jax.experimental.pallas import tpu as pltpu
from jax.sharding import PartitionSpec as P

MESH = pl.DeviceIdType.MESH
F32 = jnp.float32
BF16 = jnp.bfloat16
WAYS = ((1, 0), (-1, 0), (0, 1), (0, -1), (1, 1), (1, -1), (-1, 1), (-1, -1))
R = 32
ROWS = 10
HALF = R // 2


def mm(a, b):
    return lax.dot_general(a, b, (((1,), (0,)), ((), ())), preferred_element_type=F32)


def mm_nt(a, b):
    return lax.dot_general(a, b, (((1,), (1,)), ((), ())), preferred_element_type=F32)


def iota(shape, dim):
    return lax.broadcasted_iota(jnp.int32, shape, dim)


def z_copies(v):
    lane = iota(v.shape, 1)
    less = jnp.where(lane == 0, jnp.zeros_like(v), pltpu.roll(v, 1, 1))
    more = jnp.where(lane == 127, jnp.zeros_like(v), pltpu.roll(v, 127, 1))
    return less, v, more


def spread(factor_t):
    repeat = (iota((8 * R, R), 0) % R == iota((8 * R, R), 1)).astype(BF16)
    rows = mm(repeat, factor_t).astype(BF16)
    widen = (iota((128, 1024), 1) // 8 == iota((128, 1024), 0)).astype(BF16)
    wide = mm(rows, widen)
    keep = iota((8 * R, 1024), 1) % 8 == iota((8 * R, 1024), 0) // R
    return jnp.where(keep, wide, 0.0).astype(BF16)


def spread_t(factor_t):
    lift = (iota((1024, 128), 0) // 8 == iota((1024, 128), 1)).astype(BF16)
    repeat = (iota((8 * R, R), 0) % R == iota((8 * R, R), 1)).astype(BF16)
    rows = mm(repeat, factor_t).astype(BF16)
    tall = mm_nt(lift, rows)
    keep = iota((1024, 8 * R), 0) % 8 == iota((1024, 8 * R), 1) // R
    return jnp.where(keep, tall, 0.0).astype(BF16)


def fold(g):
    keep = iota(g.shape, 0) % 8 == iota(g.shape, 1) // R
    g = jnp.where(keep, g, 0.0)
    g = g[:, :128] + g[:, 128:]
    g = jnp.sum(g.reshape(128, 8, 128), axis=1)
    g = g + pltpu.roll(g, 64, 1)
    g = g + pltpu.roll(g, 32, 1)
    return jnp.transpose(g)[:R]


def kernel(dims, act, cot, inf, core, outf, gact_v, gcore, gin, gout,
           act_v, cot_v, a2, c2, xs_r, xs_g, red, gmu, hx_r, hx_g, hy_r, hy_g, hxs, hys,
           t_s, w32, w_f, w_b, y32, wk_i, wk_o, wk_t, acc_m, acc_b, own, part, rs_recv, y_recv, fin, part2, c_recv, xz_recv, y2_recv,
           in_sem, send_sem, recv_sem, ar_sem, f_sem, known):
    n_gx, n_gy = dims
    n_x, n_z = n_gx // 2, n_gy // 4
    group = n_x * n_z * 2
    per = R // group
    gx, gy = lax.axis_index("gx"), lax.axis_index("gy")
    x, y_lo = gx // 2, gx % 2
    z, y_hi, cr = gy // 4, (gy // 2) % 2, gy % 2
    me = (x * n_z + z) * 2 + cr
    my_y = y_hi * 2 + y_lo

    def by_y(j):
        return x * 2 + j % 2, z * 4 + (j // 2) * 2 + cr

    pairs = ((0, 7), (1, 2), (3, 4), (5, 6))
    loads = []
    for n, (src, dst) in enumerate(((cot, cot_v), (act, act_v))):
        mine = []
        for k, xx in enumerate((pl.ds(0, 1), pl.ds(7, 1), pl.ds(1, 6))):
            c = pltpu.make_async_copy(src.at[:, xx], dst.at[:, xx], in_sem.at[n, k])
            c.start()
            mine.append(c)
        loads.append(mine)

    for ref in (hx_r, hx_g, hy_r, hy_g):
        ref[...] = jnp.zeros(ref.shape, BF16)
    barrier = pltpu.get_barrier_semaphore()
    flip = 1 - 2 * cr
    has_up, has_down = z < n_z - 1, z > 0
    first, last = gy == 0, gy == n_gy - 1

    def greet(sem, partners):
        due = 0
        for there, dx, dy in partners:
            who = ((gx + dx + n_gx) % n_gx, gy + dy)
            if there is True:
                pl.semaphore_signal(sem, inc=1, device_id=who, device_id_type=MESH)
                due = due + 1
            else:

                @pl.when(there)
                def _():
                    pl.semaphore_signal(sem, inc=1, device_id=who, device_id_type=MESH)

                due = due + there.astype(jnp.int32)
        return due

    side_l, side_h = 1 - 2 * y_lo, 2 - 4 * y_hi
    up, down = jnp.logical_not(last), jnp.logical_not(first)
    near = [(True if dy == 0 else up if dy > 0 else down, dx, dy) for dx, dy in WAYS]
    near += [(True, dx, dy) for dx in (2, -2) for dy in (0, flip)]
    near += [(has_up, 0, 4), (has_up, 0, 4 + flip), (has_down, 0, -4), (has_down, 0, -4 + flip)]
    near += [(True, dx, dy + dc) for dx, dy in ((side_l, 0), (0, side_h), (side_l, side_h)) for dc in (0, flip)]
    near_due = greet(barrier, near)

    wk_o[...] = spread(outf[...])
    for ref in (xs_r, red):
        ref[:, 0:128] = jnp.zeros((ref.shape[0], 128), BF16)
        ref[:, 1152:1280] = jnp.zeros((ref.shape[0], 128), BF16)
    xs_g[:, 0:128] = jnp.zeros((768, 128), BF16)
    xs_g[:, 1152:1280] = jnp.zeros((768, 128), BF16)
    red[0:32, 128:1152] = jnp.zeros((32, 1024), BF16)
    red[288:320, 128:1152] = jnp.zeros((32, 1024), BF16)

    def inside(gxx, gyy):
        return (gxx >= 0) & (gxx < n_gx) & (gyy >= 0) & (gyy < n_gy)

    def send_copy(field, way):
        dx, dy = WAYS[way]
        src, row0, lane0, hx, hy = (gmu, 0, 0, hx_g, hy_g) if field == 0 else (red, 32, 128, hx_r, hy_r)
        edge_x = lane0 + (896 if dx > 0 else 0)
        edge_y = row0 + (224 if dy > 0 else 0)
        if dy == 0:
            s = src.at[pl.ds(row0, 256), pl.ds(edge_x, 128)]
            d = hx.at[0 if dx > 0 else 1]
        elif dx == 0:
            s = src.at[pl.ds(edge_y, 32), pl.ds(lane0, 1024)]
            d = hy.at[0 if dy > 0 else 1, :, pl.ds(128, 1024)]
        else:
            s = src.at[pl.ds(edge_y, 32), pl.ds(edge_x, 128)]
            d = hy.at[0 if dy > 0 else 1, :, pl.ds(0 if dx > 0 else 1152, 128)]
        return pltpu.make_async_remote_copy(
            src_ref=s, dst_ref=d, send_sem=send_sem.at[field, way], recv_sem=recv_sem.at[field, way],
            device_id=((gx + dx + n_gx) % n_gx, (gy + dy + n_gy) % n_gy), device_id_type=MESH)

    def send(field, way):
        dx, dy = WAYS[way]

        @pl.when(inside(gx + dx, gy + dy))
        def _():
            send_copy(field, way).start()

    def arrive(field, way):
        dx, dy = WAYS[way]

        @pl.when(inside(gx - dx, gy - dy))
        def _():
            send_copy(field, way).wait_recv()

    def sent(field, way):
        dx, dy = WAYS[way]

        @pl.when(inside(gx + dx, gy + dy))
        def _():
            send_copy(field, way).wait_send()

    for field, (raw, flat, wk, xs) in enumerate(((cot_v, c2, wk_o, xs_g), (act_v, a2, wk_i, xs_r))):
        if field == 1:
            wk_i[...] = spread(inf[...])
        for n, p in enumerate(pairs):
            for c in loads[field][0:2] if n == 0 else loads[field][2:3] if n == 1 else ():
                c.wait()
            for xx in p:
                flat[:, xx * 128:xx * 128 + 128] = raw[:, xx].astype(F32).reshape(1024, 128).astype(BF16)
            both = jnp.concatenate([flat[:, xx * 128:xx * 128 + 128] for xx in p], axis=1)
            r = mm(wk[...], both)
            for side, xx in enumerate(p):
                v = r[:, side * 128:side * 128 + 128].astype(BF16)
                copies = z_copies(v)
                if field == 0:
                    gmu[:, xx * 128:xx * 128 + 128] = copies[1]
                else:
                    red[32:288, xx * 128 + 128:xx * 128 + 256] = copies[1]
                for yy in range(8):
                    for e in range(3):
                        xs[yy * 96 + e * 32:yy * 96 + e * 32 + 32, xx * 128 + 128:xx * 128 + 256] = copies[e][yy * 32:yy * 32 + 32]
            if n == 0:
                if field == 0:
                    pl.semaphore_wait(barrier, near_due)
                    known_due = greet(known.at[0], [(True, 2, 0), (True, -2, 0), (has_up, 0, 4), (has_down, 0, -4)])
                send(field, 0)
                send(field, 1)
        for way in range(2, 8):
            send(field, way)

    pl.semaphore_wait(known.at[0], known_due)
    known_due = greet(known.at[1], [(z < n_z - 2, 0, 8), (z > 1, 0, -8)])

    eye = (iota((R, R), 0) == iota((R, R), 1)).astype(BF16)
    w32[...] = jnp.zeros(w32.shape, F32)
    for n, w in enumerate((w_f, w_b)):
        for a in range(3):
            if n == 0:
                for b in range(3):
                    for e in range(3):
                        t_s[:, (b * 3 + e) * 32:(b * 3 + e) * 32 + 32] = core[a, b, e].astype(F32)
            else:
                blocks = [core[2 - a, 2 - b, 2 - e] for b in range(3) for e in range(3)]
                t_s[:, 0:288] = mm_nt(eye, jnp.concatenate(blocks, axis=0))
            for yy in range(8):
                lo = 96 if yy == 0 else 0
                hi = 192 if yy == 7 else 288
                at = a * 768 + 96 * (yy - 1) + lo
                w32[yy * 32:yy * 32 + 32, at:at + hi - lo] = t_s[:, lo:hi]
            y32[n, 0, :, a * 96:a * 96 + 96] = t_s[:, 0:96]
            y32[n, 1, :, a * 96:a * 96 + 96] = t_s[:, 192:288]
        w[...] = w32[...].astype(BF16)
    wk_t[...] = spread_t(inf[...])

    for w, xs, acc in ((w_b, xs_g, acc_b), (w_f, xs_r, acc_m)):
        for t in range(4):
            k = jnp.concatenate([xs[:, (a + 2 * t) * 128:(a + 2 * t) * 128 + 256] for a in range(3)], axis=0)
            acc[:, t * 256:t * 256 + 256] = mm(w[...], k)
    pl.semaphore_wait(known.at[1], known_due)
    known_due = greet(known.at[2], [(True, 2, 0), (True, -2, 0), (True, 4, 0)])
    g = jnp.zeros((192, 384), F32)
    for p in range(4):
        k = jnp.concatenate([red[64 * p:64 * p + 128, a * 128:a * 128 + 1024] for a in range(3)], axis=0)
        g = g + mm_nt(xs_g[192 * p:192 * p + 192, 128:1152], k)
    for a in range(3):
        second = pltpu.roll(g[96:192, a * 128:a * 128 + 128], 96, 1)
        own[a] = g[0:96, a * 128:a * 128 + 128] + second

    def halo_x(field, hx):
        for way in range(2):
            arrive(field, way)
        for side in range(2):
            copies = z_copies(hx[side])
            for yy in range(8):
                for e in range(3):
                    hxs[side, yy * 96 + e * 32:yy * 96 + e * 32 + 32, :] = copies[e][yy * 32:yy * 32 + 32]

    def halo_y(field, hy):
        for way in range(2, 8):
            arrive(field, way)
        for side in range(2):
            for xp in range(10):
                copies = z_copies(hy[side, :, xp * 128:xp * 128 + 128])
                for e in range(3):
                    hys[side, e * 32:e * 32 + 32, xp * 128:xp * 128 + 128] = copies[e]

    def correct_x(w, acc):
        for side in range(2):
            at = 896 * side
            acc[:, at:at + 128] += mm(w[:, 1536 * side:1536 * side + 768], hxs[side])

    def correct_y(n, acc):
        for side in range(2):
            k = jnp.concatenate([hys[side, :, a * 128:a * 128 + 1024] for a in range(3)], axis=0)
            acc[224 * side:224 * side + 32, :] += mm(y32[n, side, :, 0:288].astype(BF16), k)
        return acc[...].astype(BF16)

    halo_x(0, hx_g)
    correct_x(w_b, acc_b)
    g_x = []
    for side in range(2):
        lanes = pl.ds(128 + 896 * side, 128)
        g_x.append(sum(mm_nt(hxs[side, 192 * p:192 * p + 192, :], red[64 * p:64 * p + 128, lanes]) for p in range(4)))
    halo_y(0, hy_g)
    g_y = jnp.zeros((288, 128), F32)
    for side in range(2):
        k = jnp.concatenate([hys[side, :, (2 - a) * 128:(2 - a) * 128 + 1024] for a in range(3)], axis=0)
        row = red[32 + 224 * side:64 + 224 * side, 128:1152]
        none = jnp.zeros_like(row)
        row = jnp.concatenate([none, none, row, none] if side == 0 else [row, none, none, none], axis=0)
        g_y = g_y + mm_nt(k, row)
    for a in range(3):
        total = own[a] + g_y[a * 96:a * 96 + 96]
        if a != 1:
            gxx = g_x[0] if a == 2 else g_x[1]
            total = total + gxx[0:96] + pltpu.roll(gxx[96:192], 96, 1)
        for e in range(3):
            part[:, a * 3 + 2 - e, :] = total[e * 32:e * 32 + 32]

    def wait_all(ref, sem):
        pltpu.make_async_copy(ref, ref, sem).wait()

    def start_y(buf, n):
        for k in range(1, 4):
            pltpu.make_async_remote_copy(
                src_ref=buf.at[my_y], dst_ref=buf.at[my_y], send_sem=ar_sem.at[n], recv_sem=ar_sem.at[n + 1],
                device_id=by_y((my_y + k) % 4), device_id_type=MESH).start()

    def member(k):
        q = k // 2
        there_x, there_z, there_c = (x + n_x // 2 + q // n_z) % n_x, (z + n_z // 2 + q) % n_z, (cr + k) % 2
        return (there_x * n_z + there_z) * 2 + there_c, (there_x * 2 + y_lo, there_z * 4 + y_hi * 2 + there_c)

    myself = 2 * ((n_x // 2) * n_z + n_z // 2)

    def each_member(body):
        lax.fori_loop(0, myself, body, 0)
        lax.fori_loop(myself + 1, group, body, 0)

    def start_rs(k, c):
        j, who = member(k)
        slot = jnp.where(k < myself, k, k - 1)
        pltpu.make_async_remote_copy(
            src_ref=part.at[pl.ds(j * per, per)], dst_ref=rs_recv.at[slot], send_sem=ar_sem.at[0], recv_sem=ar_sem.at[1],
            device_id=who, device_id_type=MESH).start()
        return c

    def start_ag(k, c):
        pltpu.make_async_remote_copy(
            src_ref=fin.at[pl.ds(me * per, per)], dst_ref=fin.at[pl.ds(me * per, per)], send_sem=ar_sem.at[4], recv_sem=ar_sem.at[5],
            device_id=member(k)[1], device_id_type=MESH).start()
        return c

    other = (gx, gy + 1 - 2 * cr)
    mine, theirs = pl.ds(pl.multiple_of(cr * HALF, HALF), HALF), pl.ds(pl.multiple_of((1 - cr) * HALF, HALF), HALF)
    plane = n_x * n_z
    at = x * n_z + z
    results = (gin, gout)

    def to_core(n):
        return pltpu.make_async_remote_copy(
            src_ref=part2.at[n, theirs], dst_ref=c_recv.at[n], send_sem=f_sem.at[n, 0], recv_sem=f_sem.at[n, 1],
            device_id=other, device_id_type=MESH)

    def over_xz(n):
        to_core(n).wait_recv()
        xz_recv[n, at] = part2[n, mine] + c_recv[n]

        def start_xz(k, c):
            there_x, there_z = (x + n_x // 2 + k // n_z) % n_x, (z + n_z // 2 + k) % n_z
            pltpu.make_async_remote_copy(
                src_ref=xz_recv.at[n, at], dst_ref=xz_recv.at[n, at], send_sem=f_sem.at[n, 2], recv_sem=f_sem.at[n, 3],
                device_id=(there_x * 2 + y_lo, there_z * 4 + y_hi * 2 + cr), device_id_type=MESH).start()
            return c

        lax.fori_loop(0, myself // 2, start_xz, 0)
        lax.fori_loop(myself // 2 + 1, plane, start_xz, 0)

    def over_y(n):
        wait_all(xz_recv.at[n, pl.ds(0, plane - 1)], f_sem.at[n, 3])
        y2_recv[n, my_y * 2 + cr] = jnp.sum(xz_recv[n], axis=0)
        for k in range(1, 8):
            to_y = (my_y + k // 2) % 4
            who = (x * 2 + to_y % 2, z * 4 + (to_y // 2) * 2 + (cr + k) % 2)
            pltpu.make_async_remote_copy(
                src_ref=y2_recv.at[n, my_y * 2 + cr], dst_ref=y2_recv.at[n, my_y * 2 + cr],
                send_sem=f_sem.at[n, 4], recv_sem=f_sem.at[n, 5], device_id=who, device_id_type=MESH).start()

    def back(n):
        wait_all(y2_recv.at[n, pl.ds(0, 7)], f_sem.at[n, 5])
        halves = [(y2_recv[n, c] + y2_recv[n, 2 + c]) + (y2_recv[n, 4 + c] + y2_recv[n, 6 + c]) for c in range(2)]
        results[n][...] = jnp.concatenate(halves, axis=0)

    gr = correct_y(1, acc_b)
    part[:, 9, :] = fold(mm_nt(a2[...], gr))
    pl.semaphore_wait(known.at[2], known_due)
    each_member(start_rs)

    halo_x(1, hx_r)
    correct_x(w_f, acc_m)
    halo_y(1, hy_r)
    mixed = correct_y(0, acc_m)
    part2[1] = fold(mm_nt(c2[...], mixed))
    to_core(1).start()
    for t in range(4):
        r = mm(wk_t[...], gr[:, t * 256:t * 256 + 256])
        for side in range(2):
            gact_v[:, 2 * t + side] = r[:, side * 128:side * 128 + 128].reshape(128, 8, 128).astype(BF16)
    over_xz(1)

    wait_all(rs_recv, ar_sem.at[1])
    y_recv[my_y] = part[pl.ds(me * per, per)] + jnp.sum(rs_recv[...], axis=0)
    start_y(y_recv, 2)
    wait_all(y_recv.at[pl.ds(0, 3)], ar_sem.at[3])
    fin[pl.ds(me * per, per)] = jnp.sum(y_recv[...], axis=0)
    each_member(start_ag)
    over_y(1)
    back(1)
    wait_all(rs_recv, ar_sem.at[5])
    for a in range(3):
        for e in range(3):
            v = fin[:, a * 3 + e, :]
            for b in range(3):
                gcore[a, b, e] = v[:, b * 32:b * 32 + 32]
    wait_all(rs_recv, ar_sem.at[0])
    wait_all(y_recv.at[pl.ds(0, 3)], ar_sem.at[2])
    wait_all(rs_recv, ar_sem.at[4])
    gin[...] = fin[:, 9, :]
    for n in range(1, 2):
        to_core(n).wait_send()
        wait_all(xz_recv.at[n, pl.ds(0, plane - 1)], f_sem.at[n, 2])
        wait_all(y2_recv.at[n, pl.ds(0, 7)], f_sem.at[n, 4])
    for field in range(2):
        for way in range(8):
            sent(field, way)


def finish(*refs):
    copies = [pltpu.make_async_copy(refs[0].at[pl.ds(16 * n, 16)], refs[4].at[pl.ds(16 * n, 16)], refs[8].at[n]) for n in range(8)]
    copies += [pltpu.make_async_copy(refs[1].at[n], refs[5].at[n], refs[8].at[8 + n]) for n in range(3)]
    copies += [pltpu.make_async_copy(refs[n], refs[n + 4], refs[8].at[9 + n]) for n in range(2, 4)]
    for c in copies:
        c.start()
    for c in copies:
        c.wait()


def shards(dims, activation, cotangent, in_factor, core, out_factor):
    n_gx, n_gy = dims
    group = n_gx * n_gy // 4
    per = R // group
    vm = pl.BlockSpec(memory_space=pltpu.VMEM)
    hbm = pl.BlockSpec(memory_space=pl.ANY)
    held = pl.pallas_call(
        functools.partial(kernel, dims),
        out_shape=(
            pltpu.VMEM(activation.shape, BF16),
            pltpu.VMEM((3, 3, 3, R, R), F32),
            pltpu.VMEM((R, 128), F32),
            pltpu.VMEM((R, 128), F32),
        ),
        in_specs=[hbm, hbm, vm, vm, vm],
        out_specs=(vm, vm, vm, vm),
        scratch_shapes=[
            pltpu.VMEM((128, 8, 8, 128), BF16),
            pltpu.VMEM((128, 8, 8, 128), BF16),
            pltpu.VMEM((1024, 1024), BF16),
            pltpu.VMEM((1024, 1024), BF16),
            pltpu.VMEM((768, 1280), BF16),
            pltpu.VMEM((768, 1280), BF16),
            pltpu.VMEM((320, 1280), BF16),
            pltpu.VMEM((256, 1024), BF16),
            pltpu.VMEM((2, 256, 128), BF16),
            pltpu.VMEM((2, 256, 128), BF16),
            pltpu.VMEM((2, 32, 1280), BF16),
            pltpu.VMEM((2, 32, 1280), BF16),
            pltpu.VMEM((2, 768, 128), BF16),
            pltpu.VMEM((2, 96, 1280), BF16),
            pltpu.VMEM((32, 384), F32),
            pltpu.VMEM((256, 2304), F32),
            pltpu.VMEM((256, 2304), BF16),
            pltpu.VMEM((256, 2304), BF16),
            pltpu.VMEM((2, 2, 32, 384), F32),
            pltpu.VMEM((256, 1024), BF16),
            pltpu.VMEM((256, 1024), BF16),
            pltpu.VMEM((1024, 256), BF16),
            pltpu.VMEM((256, 1024), F32),
            pltpu.VMEM((256, 1024), F32),
            pltpu.VMEM((3, 96, 128), F32),
            pltpu.VMEM((R, ROWS, 128), F32),
            pltpu.VMEM((group - 1, per, ROWS, 128), F32),
            pltpu.VMEM((4, per, ROWS, 128), F32),
            pltpu.VMEM((R, ROWS, 128), F32),
            pltpu.VMEM((2, R, 128), F32),
            pltpu.VMEM((2, HALF, 128), F32),
            pltpu.VMEM((2, group // 2, HALF, 128), F32),
            pltpu.VMEM((2, 8, HALF, 128), F32),
            pltpu.SemaphoreType.DMA((2, 3)),
            pltpu.SemaphoreType.DMA((2, 8)),
            pltpu.SemaphoreType.DMA((2, 8)),
            pltpu.SemaphoreType.DMA((10,)),
            pltpu.SemaphoreType.DMA((2, 6)),
            pltpu.SemaphoreType.REGULAR((3,)),
        ],
        compiler_params=pltpu.CompilerParams(collective_id=0, has_side_effects=True, vmem_limit_bytes=60 * 1024 * 1024),
    )(activation, cotangent, in_factor.T, core, out_factor.T)
    gact, gcore, gin, gout = pl.pallas_call(
        finish,
        out_shape=(
            jax.ShapeDtypeStruct(activation.shape, BF16),
            jax.ShapeDtypeStruct((3, 3, 3, R, R), F32),
            jax.ShapeDtypeStruct((R, 128), F32),
            jax.ShapeDtypeStruct((R, 128), F32),
        ),
        in_specs=[vm] * 4,
        out_specs=(hbm,) * 4,
        scratch_shapes=[pltpu.SemaphoreType.DMA((13,))],
        compiler_params=pltpu.CompilerParams(vmem_limit_bytes=24 * 1024 * 1024),
    )(*held)
    return gact, gin.T, gcore, gout.T


def solution(mesh):
    dims = (mesh.shape["gx"], mesh.shape["gy"])
    placed = (P(None, "gx", "gy", None), P(None, "gx", "gy", None), P(), P(), P())
    return jax.shard_map(
        functools.partial(shards, dims),
        mesh=mesh,
        in_specs=placed,
        out_specs=(P(None, "gx", "gy", None), P(), P(), P()),
        check_vma=False,
    )
```
